512 devices in a mesh: space: 64 (over x, z, core), chan: 8 (over y).
Axes of the slice: x: 4, y: 8, z: 8, core: 2. Of those that a mesh axis runs over, the one named last changes fastest.
Arguments:
- features: bfloat16 [256, 128, 512], P(None, 'space'), may hold values from -12 to 17
- first_weight: bfloat16 [27, 256, 256], P(None, 'chan'), may hold values from -0.078125 to 0.078125
- first_gain: float32 [256], P('chan'), may hold values from 0.5 to 1.5
- first_bias: float32 [256], P('chan'), may hold values from -3 to 3
- down_weight: bfloat16 [27, 320, 256], P(None, None, 'chan'), may hold values from -0.078125 to 0.078125
- down_gain: float32 [320], P('chan'), may hold values from 0.5 to 1.5
- down_bias: float32 [320], P('chan'), may hold values from -3 to 3
- third_weight: bfloat16 [27, 320, 320], P(None, 'chan'), may hold values from -0.0625 to 0.0625
- third_gain: float32 [320], P('chan'), may hold values from 0.5 to 1.5
- third_bias: float32 [320], P('chan'), may hold values from -3 to 3
Outputs:
- bottleneck: bfloat16 [320, 64, 128], P('chan', 'space')
The draws below stay inside these ranges and needn't reach their ends.
All inputs are finite; a program needn't handle non-finite values.
Results may differ from the reference program's by a relative error of at most 0.027.
Values may be sent and summed in bfloat16 or wider, within the bound.
No kernel may reach another device: no remote copies, remote signals or barrier semaphores. Data moves between devices by JAX's collectives and lax.ppermute only.
A program may use at most 64 MiB of HBM per device.

```python
import jax
import jax.numpy as jnp
from jax import lax

CH_IN = 256
CH = 320
ROWS = 16
COLS = 32
D4 = 128
P4 = 512


def draw_features(key, part):
    key = jax.random.fold_in(key, 11)
    noise_key, offset_key = jax.random.split(key, 2)
    position = jnp.arange(D4, dtype=jnp.float32) / max(D4 - 1, 1)
    ramp = 10.0 ** position
    noise = jnp.clip(jax.random.normal(noise_key, (CH_IN, D4, P4), jnp.float32), -4.0, 4.0)
    offset = jax.random.uniform(offset_key, (CH_IN, 1, 1), jnp.float32, 0.5, 1.5)
    values = 0.3 * ramp[None, :, None] * (noise + offset)
    return values.astype(jnp.bfloat16)


def block_scale(stream_key, shape, cuts, smallest, top_value):
    level, own = 1.0, jax.random.fold_in(stream_key, 6)
    for dim, blocks in cuts:
        heights = jnp.exp(jax.random.uniform(jax.random.fold_in(own, dim), (blocks,), jnp.float32, smallest / len(cuts), top_value / len(cuts)))
        level = level * jnp.repeat(heights, shape[dim] // blocks).reshape([-1 if axis == dim else 1 for axis in range(len(shape))])
    return level


def bell_draw(rng, dims, width, bound, pieces=(), held_as=jnp.bfloat16):
    array = width * jax.random.normal(rng, dims, jnp.float32)
    if pieces:
        array = array * block_scale(rng, dims, pieces, -0.22, 0.18)
    return jnp.clip(array, -bound, bound).astype(held_as)


def setup_inputs(seed: int = 0) -> dict:
    streams_of = jax.random.split(jax.random.key(seed), 11)
    return {
        "features": draw_features(jax.random.fold_in(streams_of[10], 71), 0),
        "first_weight": bell_draw(streams_of[1], (27, CH_IN, CH_IN), (27 * CH_IN) ** -0.5, 0.078125, ((1, 8),)),
        "first_gain": jnp.clip(1.0 + 0.1 * jax.random.normal(streams_of[2], (CH_IN,), jnp.float32), 0.5, 1.5),
        "first_bias": bell_draw(streams_of[3], (CH_IN,), 0.5, 3.0, ((0, 8),), jnp.float32),
        "down_weight": bell_draw(streams_of[4], (27, CH, CH_IN), (27 * CH_IN) ** -0.5, 0.078125, ((2, 8),)),
        "down_gain": jnp.clip(1.0 + 0.1 * jax.random.normal(streams_of[5], (CH,), jnp.float32), 0.5, 1.5),
        "down_bias": bell_draw(streams_of[6], (CH,), 0.5, 3.0, ((0, 8),), jnp.float32),
        "third_weight": bell_draw(streams_of[7], (27, CH, CH), (27 * CH) ** -0.5, 0.0625, ((1, 8),)),
        "third_gain": jnp.clip(1.0 + 0.1 * jax.random.normal(streams_of[8], (CH,), jnp.float32), 0.5, 1.5),
        "third_bias": bell_draw(streams_of[9], (CH,), 0.5, 3.0, ((0, 8),), jnp.float32),
    }


EPSILON = 1e-05
SLOPE = 0.01

def convolve(volume, weight, stride, row_count, col_count):
    chan_count, depth_count, cell_count = volume.shape
    lhs_volume = volume.astype(jnp.float32).reshape(1, chan_count, depth_count, row_count, col_count)
    kernel = weight.astype(jnp.float32).reshape(3, 3, 3, weight.shape[1], weight.shape[2]).transpose(3, 4, 0, 1, 2)
    result = lax.conv_general_dilated(lhs_volume, kernel, (stride, stride, stride), ((1, 1), (1, 1), (1, 1)), dimension_numbers=('NCDHW', 'OIDHW', 'NCDHW'), precision=lax.Precision.HIGHEST)
    return result.reshape(weight.shape[1], result.shape[2], result.shape[3] * result.shape[4])

def normalize(summed, gain, bias):
    average = lax.optimization_barrier(jnp.mean(summed, axis=(1, 2), keepdims=True))
    centred = summed - average
    spread = lax.optimization_barrier(jnp.mean(centred * centred, axis=(1, 2), keepdims=True))
    scaled = gain[:, None, None] * centred * lax.rsqrt(spread + EPSILON) + bias[:, None, None]
    return jnp.where(scaled >= 0, scaled, SLOPE * scaled).astype(jnp.bfloat16)

def reference(features, first_weight, first_gain, first_bias, down_weight, down_gain, down_bias, third_weight, third_gain, third_bias):
    level = normalize(convolve(features, first_weight, 1, ROWS, COLS), first_gain, first_bias)
    bottom = normalize(convolve(level, down_weight, 2, ROWS, COLS), down_gain, down_bias)
    return normalize(convolve(bottom, third_weight, 1, ROWS // 2, COLS // 2), third_gain, third_bias)
```

```python
import jax
import jax.numpy as jnp
from jax import lax
from jax.sharding import PartitionSpec as P

COLS = 32


EPSILON = 1e-05
SLOPE = 0.01


def extended(block, sides, width):
    for axis, dim in sides:
        count = lax.axis_size(axis)
        forward = [(i, i + 1) for i in range(count - 1)]
        backward = [(target, source) for source, target in forward]
        low = lax.ppermute(
            lax.slice_in_dim(block, block.shape[dim] - width, None, axis=dim), axis, forward
        )
        high = lax.ppermute(lax.slice_in_dim(block, 0, width, axis=dim), axis, backward)
        block = jnp.concatenate([low, block, high], axis=dim)
    return block


def from_behind(value, axis, by):
    count = lax.axis_size(axis)
    pairs = [(i, i + by) for i in range(count) if 0 <= i + by < count]
    return lax.ppermute(value, axis, pairs)


def shifted(volume, row_step, col_step, col_count):
    cell_count = volume.shape[2]
    margin = col_count + 1
    padded = jnp.pad(volume, ((0, 0), (0, 0), (margin, margin)))
    offset = margin + row_step * col_count + col_step
    moved_cells = lax.slice_in_dim(padded, offset, offset + cell_count, axis=2)
    column = jnp.arange(cell_count, dtype=jnp.int32) % col_count + col_step
    inside = (column >= 0) & (column < col_count)
    return jnp.where(inside, moved_cells, jnp.zeros((), moved_cells.dtype))


def convolve_same(padded, weight, col_count):
    depth_count = padded.shape[1] - 2
    summed = jnp.zeros((weight.shape[1], depth_count, padded.shape[2]), jnp.float32)
    for row_tap in range(3):
        for col_tap in range(3):
            moved_cells = shifted(padded, row_tap - 1, col_tap - 1, col_count)
            for depth_tap in range(3):
                kernel = weight[depth_tap * 9 + row_tap * 3 + col_tap]
                summed = summed + jnp.einsum(
                    "oi,izp->ozp",
                    kernel,
                    moved_cells[:, depth_tap : depth_tap + depth_count],
                    preferred_element_type=jnp.float32,
                )
    return summed


def phase_split(volume, col_count):
    chan_count, depth_count, cell_count = volume.shape
    lattice = volume.reshape(
        chan_count, depth_count, cell_count // (2 * col_count), 2, col_count // 2, 2
    )
    return [
        [
            lattice[:, :, :, row_phase, :, col_phase].reshape(
                chan_count, depth_count, cell_count // 4
            )
            for col_phase in range(2)
        ]
        for row_phase in range(2)
    ]


def down_taps(layers, col_count):
    taps = []
    for depth_tap in range(3):
        phases = phase_split(layers[depth_tap], col_count)
        for row_tap in range(3):
            for col_tap in range(3):
                source = phases[(row_tap + 1) % 2][(col_tap + 1) % 2]
                taps.append(
                    shifted(
                        source, -1 if row_tap == 0 else 0, -1 if col_tap == 0 else 0, col_count // 2
                    )
                )
    return taps


def everyone(row, axis):
    count = lax.axis_size(axis)
    copies = jnp.broadcast_to(row[None], (count,) + row.shape)
    return lax.all_to_all(copies, axis, 0, 0, tiled=True)


def normalize(summed, gain, bias):
    chan_count = summed.shape[0]
    average = jnp.mean(summed, axis=(1, 2))
    centred = summed - average[:, None, None]
    spread = jnp.mean(centred * centred, axis=(1, 2))
    row = jnp.pad(jnp.concatenate([average, spread])[None], ((0, 0), (0, 128 - 2 * chan_count)))
    rows = everyone(row, "space")[:, 0]
    averages = rows[:, :chan_count]
    average = jnp.mean(averages, axis=0)
    spread = jnp.mean(rows[:, chan_count : 2 * chan_count], axis=0) + jnp.mean(
        (averages - average[None]) ** 2, axis=0
    )
    scaled = (
        gain[:, None, None]
        * (summed - average[:, None, None])
        * lax.rsqrt(spread[:, None, None] + EPSILON)
        + bias[:, None, None]
    )
    return jnp.where(scaled >= 0, scaled, SLOPE * scaled).astype(jnp.bfloat16)


def local(
    features,
    first_weight,
    first_gain,
    first_bias,
    down_weight,
    down_gain,
    down_bias,
    third_weight,
    third_gain,
    third_bias,
):
    framed = extended(features, (("space", 1),), 1)
    first = convolve_same(framed, first_weight, COLS)
    level = normalize(first, first_gain, first_bias)
    even_slices = level[:, 0::2]
    odd_slices = level[:, 1::2]
    blank = jnp.zeros_like(level[:, :1])
    layers = (
        jnp.concatenate([blank, odd_slices], axis=1),
        jnp.concatenate([even_slices, blank], axis=1),
        jnp.concatenate([odd_slices, blank], axis=1),
    )
    taps = down_taps(layers, COLS)
    summed = jnp.zeros(
        (down_weight.shape[1] // lax.axis_size("chan") * lax.axis_size("chan"),)
        + taps[0].shape[1:],
        jnp.float32,
    )
    for tap_number in range(27):
        summed = summed + jnp.einsum(
            "oi,izp->ozp",
            down_weight[tap_number],
            taps[tap_number],
            preferred_element_type=jnp.float32,
        )
    chans = lax.axis_size("chan")
    parts = summed.astype(jnp.bfloat16).reshape(
        (chans, summed.shape[0] // chans) + summed.shape[1:]
    )
    reduced = jnp.sum(
        lax.all_to_all(parts, "chan", 0, 0, tiled=True).astype(jnp.float32), axis=0
    )
    carried = from_behind(reduced[:, -1:], "space", 1)
    reduced = jnp.concatenate([reduced[:, :1] + carried, reduced[:, 1:-1]], axis=1)
    bottom = normalize(reduced, down_gain, down_bias)
    gathered = everyone(bottom, "chan").reshape((-1,) + bottom.shape[1:])
    padded = extended(gathered, (("space", 1),), 1)
    third = convolve_same(padded, third_weight, COLS // 2)
    return normalize(third, third_gain, third_bias)


def solution(mesh):
    return jax.shard_map(
        local,
        mesh=mesh,
        in_specs=(
            P(None, "space", None),
            P(None, "chan", None),
            P("chan"),
            P("chan"),
            P(None, None, "chan"),
            P("chan"),
            P("chan"),
            P(None, "chan", None),
            P("chan"),
            P("chan"),
        ),
        out_specs=P("chan", "space", None),
        check_vma=False,
    )
```

```python
import jax
import jax.numpy as jnp
from jax import lax
from jax.experimental import pallas as pl
from jax.experimental.pallas import tpu as pltpu
from jax.sharding import PartitionSpec as P

ROWS = 16
COLS = 32
CELLS = ROWS * COLS
HALF_ROWS = ROWS // 2
HALF_COLS = COLS // 2
HALF_CELLS = HALF_ROWS * HALF_COLS
LANES = 128
PAIR = 48
AFFINE_ROWS = 16
EPSILON = 1e-05
SLOPE = 0.01

VMEM = pl.BlockSpec(memory_space=pltpu.VMEM)


def kernel_call(body, outputs, operands, flops, name):
    return pl.pallas_call(
        body,
        out_shape=outputs,
        in_specs=[VMEM] * len(operands),
        out_specs=jax.tree.map(lambda _: VMEM, outputs),
        compiler_params=pltpu.CompilerParams(vmem_limit_bytes=32 * 1024 * 1024),
        cost_estimate=pl.CostEstimate(flops=flops, bytes_accessed=2 << 20, transcendentals=0),
        name=name,
    )(*operands)


def iota(shape, dim):
    return lax.broadcasted_iota(jnp.int32, shape, dim)


def dot(a, b):
    return jnp.dot(a, b, preferred_element_type=jnp.float32)


def dot_nt(a, b):
    return lax.dot_general(a, b, (((1,), (1,)), ((), ())), preferred_element_type=jnp.float32)


def to_row(column, offset):
    n = column.shape[0]
    hit = iota((n, LANES), 1) == iota((n, LANES), 0) + offset
    return jnp.sum(jnp.where(hit, column, 0.0), axis=0, keepdims=True)


def to_column(row, offset, n):
    width = row.shape[1]
    hit = iota((n, width), 1) == iota((n, width), 0) + offset
    return jnp.sum(jnp.where(hit, row, 0.0), axis=1, keepdims=True)


def shift_add(taps, out_chans, row_count, col_count):
    cells = row_count * col_count
    block = 3 * out_chans
    cell = iota((block, cells), 1)
    above = pltpu.roll(taps[:block], col_count, axis=1)
    below = pltpu.roll(taps[2 * block :], cells - col_count, axis=1)
    rows = (
        taps[block : 2 * block]
        + jnp.where(cell >= col_count, above, 0.0)
        + jnp.where(cell < cells - col_count, below, 0.0)
    )
    column = iota((out_chans, cells), 1) % col_count
    left = pltpu.roll(rows[:out_chans], 1, axis=1)
    right = pltpu.roll(rows[2 * out_chans :], cells - 1, axis=1)
    return (
        rows[out_chans : 2 * out_chans]
        + jnp.where(column != 0, left, 0.0)
        + jnp.where(column != col_count - 1, right, 0.0)
    )


def leaky(value):
    return jnp.where(value >= 0, value, SLOPE * value)


def send_kernel(features_ref, weight_ref, slices_ref, send_ref):
    chans = features_ref.shape[0]
    pairs = features_ref[...].reshape(2 * chans, CELLS)
    for j in range(2):
        pick = (iota((chans, 2 * chans), 1) == 2 * iota((chans, 2 * chans), 0) + j).astype(
            jnp.bfloat16
        )
        slices_ref[j] = dot(pick, pairs).astype(jnp.bfloat16)
    block = weight_ref.shape[0] // 3
    out_chans = block // 9
    lower, upper = slices_ref[0], slices_ref[1]
    tap0, tap1 = weight_ref[:block], weight_ref[block : 2 * block]
    send_ref[0] = shift_add(dot(tap0, lower) + dot(tap1, upper), out_chans, ROWS, COLS)
    send_ref[1] = shift_add(dot(tap0, upper), out_chans, ROWS, COLS)


def own_kernel(
    slices_ref, weight_ref, third_ref, gain_ref, bias_ref,
    own_ref, select_ref, stacked_ref, affine_ref,
):
    block = weight_ref.shape[0] // 3
    out_chans = block // 9
    lower, upper = slices_ref[0], slices_ref[1]
    tap1, tap2 = weight_ref[block : 2 * block], weight_ref[2 * block :]
    own_ref[0] = shift_add(dot(tap2, lower), out_chans, ROWS, COLS)
    own_ref[1] = shift_add(dot(tap1, lower) + dot(tap2, upper), out_chans, ROWS, COLS)

    place = iota((HALF_CELLS, CELLS), 0)
    cell = iota((HALF_CELLS, CELLS), 1)
    row, column = cell // COLS, cell % COLS
    row_gap = row - 2 * (place // HALF_COLS)
    column_gap = column - 2 * (place % HALF_COLS)
    for tap in range(9):
        hit = (row_gap == tap // 3 - 1) & (column_gap == tap % 3 - 1)
        select_ref[tap * HALF_CELLS : (tap + 1) * HALF_CELLS] = hit.astype(jnp.bfloat16)

    third_out, third_in = third_ref.shape[1:]
    stacked_ref[...] = jnp.zeros_like(stacked_ref)
    wide = stacked_ref.shape[2] // 3
    for depth in range(3):
        for tap in range(9):
            stacked_ref[tap, :third_out, depth * wide : depth * wide + third_in] = third_ref[
                depth * 9 + tap
            ]

    n = gain_ref.shape[1]
    start = lax.axis_index("chan") * n
    rows = []
    lane = iota((n, LANES), 1)
    channel = iota((n, LANES), 0) + start
    columns = [to_column(ref[...], 0, n) for ref in (gain_ref, bias_ref)]
    for column in columns:
        for k in range(2):
            hit = channel == lane + k * LANES
            rows.append(jnp.sum(jnp.where(hit, column, 0.0), axis=0, keepdims=True))
    gain_hit = channel == lane + 2 * LANES
    bias_hit = (channel == lane + 2 * LANES - LANES // 2) & (lane >= LANES // 2)
    tail = jnp.where(gain_hit, columns[0], 0.0) + jnp.where(bias_hit, columns[1], 0.0)
    rows.append(jnp.sum(tail, axis=0, keepdims=True))
    row = iota((AFFINE_ROWS, LANES), 0)
    values = jnp.zeros((AFFINE_ROWS, LANES), jnp.float32)
    for k, value in enumerate(rows):
        values = jnp.where(row == k, value, values)
    high = values.astype(jnp.bfloat16).astype(jnp.float32)
    middle = (values - high).astype(jnp.bfloat16).astype(jnp.float32)
    low = values - high - middle
    affine_ref[...] = (
        high + pltpu.roll(middle, 5, axis=0) + pltpu.roll(low, 10, axis=0)
    ).astype(jnp.bfloat16)


def total_kernel(own_ref, got_ref, first0_ref, first1_ref, copies_ref):
    at_start = lax.axis_index("space") == 0
    first0 = got_ref[0] + jnp.where(at_start, 0.0, own_ref[0])
    first1 = own_ref[1] + jnp.where(at_start, 0.0, got_ref[1])
    first0_ref[...] = first0
    first1_ref[...] = first1
    cells = 2 * CELLS
    mean = (
        jnp.sum(first0, axis=1, keepdims=True) + jnp.sum(first1, axis=1, keepdims=True)
    ) / cells
    spread = (
        jnp.sum((first0 - mean) ** 2, axis=1, keepdims=True)
        + jnp.sum((first1 - mean) ** 2, axis=1, keepdims=True)
    ) / cells
    row = to_row(mean, 0) + to_row(spread, mean.shape[0])
    copies_ref[...] = jnp.broadcast_to(row, copies_ref.shape)


def column_statistics(rows, n):
    average = jnp.mean(rows, axis=0, keepdims=True)
    apart = jnp.mean((rows - average) ** 2, axis=0, keepdims=True)
    mean = to_column(average, 0, n)
    spread = to_column(average, n, n) + to_column(apart, 0, n)
    return mean, spread


def down_kernel(
    rows_ref, first0_ref, first1_ref, first2_ref, gain_ref, bias_ref,
    select_ref, weight_ref, affine_ref, copies_ref,
):
    n = first0_ref.shape[0]
    mean, spread = column_statistics(rows_ref[...], n)
    gain = to_column(gain_ref[...], 0, n)
    bias = to_column(bias_ref[...], 0, n)
    scale = gain * lax.rsqrt(spread + EPSILON)
    at_start = lax.axis_index("space") == 0

    def level(ref):
        return leaky(scale * (ref[...] - mean) + bias)

    layers = jnp.concatenate(
        [
            jnp.where(at_start, 0.0, level(first0_ref)),
            level(first1_ref),
            level(first2_ref),
            jnp.zeros((LANES - 3 * n, CELLS), jnp.float32),
        ],
        axis=0,
    ).astype(jnp.bfloat16)
    out_chans = weight_ref.shape[1]
    picked = dot_nt(select_ref[...], layers).astype(jnp.bfloat16)
    windows, weights = [], []
    for tap in range(9):
        windows.append(picked[tap * HALF_CELLS : (tap + 1) * HALF_CELLS])
        for depth in range(3):
            at = (depth * 9 + tap) * n
            weights.append(weight_ref[at : at + n])
        weights.append(jnp.zeros((LANES - 3 * n, out_chans), jnp.bfloat16))
    parts = dot(jnp.concatenate(windows, axis=1), jnp.concatenate(weights, axis=0))
    half = HALF_CELLS // 2
    tail = parts[:, 2 * LANES :]
    packed = jnp.concatenate(
        [
            parts[:, :LANES],
            parts[:, LANES : 2 * LANES],
            jnp.concatenate([tail[:half], tail[half:]], axis=1),
        ],
        axis=0,
    ).astype(jnp.bfloat16)
    message = jnp.concatenate([packed, affine_ref[...]], axis=0)
    for c in range(copies_ref.shape[0]):
        copies_ref[c] = message


def fold(row):
    return row + pltpu.roll(row, LANES // 2, axis=1)


def reduced_kernel(parts_ref, packed_ref, affine_ref, copies_ref):
    total = parts_ref[0].astype(jnp.float32)
    for c in range(1, parts_ref.shape[0]):
        total = total + parts_ref[c].astype(jnp.float32)
    size = packed_ref.shape[0]
    packed = total[:size]
    packed_ref[...] = packed
    tail = total[size:]
    affine_ref[...] = (
        tail
        + pltpu.roll(tail, AFFINE_ROWS - 5, axis=0)
        + pltpu.roll(tail, AFFINE_ROWS - 10, axis=0)
    )
    blocks = (packed[:LANES], packed[LANES : 2 * LANES], packed[2 * LANES :])
    means, spreads = [], []
    for k, block in enumerate(blocks):
        mean = jnp.sum(block, axis=0, keepdims=True) / HALF_CELLS
        if k == 2:
            mean = fold(mean)
        spread = jnp.sum((block - mean) ** 2, axis=0, keepdims=True) / HALF_CELLS
        if k == 2:
            spread = fold(spread)
        means.append(mean)
        spreads.append(spread)
    lane = iota((1, LANES), 1)
    last = jnp.where(lane < LANES // 2, means[2], spreads[2])
    row = jnp.concatenate(means[:2] + spreads[:2] + [last], axis=1)
    copies_ref[...] = jnp.broadcast_to(row, copies_ref.shape)


def third_kernel(
    rows_ref, own_ref, before_ref, after_ref, affine_ref, stacked_ref, third_ref, copies_ref
):
    rows = rows_ref[...]
    average = jnp.mean(rows, axis=0, keepdims=True)
    apart = jnp.mean((rows - average) ** 2, axis=0, keepdims=True)
    lane = iota((1, LANES), 1)
    in_low = lane < LANES // 2

    def piece(row, k):
        return row[:, k * LANES : (k + 1) * LANES]

    def swap(row):
        return pltpu.roll(row, LANES // 2, axis=1)

    last, last_apart = piece(average, 4), piece(apart, 4)
    affine = affine_ref[...]
    gains = [affine[0:1], affine[1:2]]
    biases = [affine[2:3], affine[3:4]]
    both = affine[4:5]
    gains.append(jnp.where(in_low, both, swap(both)))
    biases.append(jnp.where(in_low, swap(both), both))
    means = [piece(average, 0), piece(average, 1), jnp.where(in_low, last, swap(last))]
    spreads = [
        piece(average, 2) + piece(apart, 0),
        piece(average, 3) + piece(apart, 1),
        jnp.where(in_low, swap(last) + last_apart, last + swap(last_apart)),
    ]
    space = lax.axis_index("space")
    here = [space != 0, None, space != lax.axis_size("space") - 1]
    size = own_ref.shape[0]
    edges = (0, LANES, 2 * LANES, size)
    columns = []
    for ref, keep in zip((before_ref, own_ref, after_ref), here):
        blocks = []
        for k in range(3):
            block = ref[edges[k] : edges[k + 1]]
            scale = gains[k] * lax.rsqrt(spreads[k] + EPSILON)
            block = leaky(scale * (block - means[k]) + biases[k])
            if keep is not None:
                block = jnp.where(keep, block, 0.0)
            blocks.append(block)
        tail = blocks[2]
        tail = jnp.concatenate([tail, pltpu.roll(tail, LANES // 2, axis=1)], axis=0)
        blocks[2] = jnp.where(iota(tail.shape, 1) < LANES // 2, tail, 0.0)
        columns += [block.astype(jnp.bfloat16) for block in blocks]
    bottom = jnp.concatenate(columns, axis=1)
    taps = dot_nt(stacked_ref[...].reshape(9 * PAIR, bottom.shape[1]), bottom)
    n = third_ref.shape[0]
    third = shift_add(taps, PAIR, HALF_ROWS, HALF_COLS)[:n]
    third_ref[...] = third
    mean = jnp.sum(third, axis=1, keepdims=True) / HALF_CELLS
    spread = jnp.sum((third - mean) ** 2, axis=1, keepdims=True) / HALF_CELLS
    row = to_row(mean, 0) + to_row(spread, n)
    copies_ref[...] = jnp.broadcast_to(row, copies_ref.shape)


def last_kernel(rows_ref, third_ref, gain_ref, bias_ref, out_ref):
    n = third_ref.shape[0]
    mean, spread = column_statistics(rows_ref[...], n)
    gain = to_column(gain_ref[...], 0, n)
    bias = to_column(bias_ref[...], 0, n)
    scale = gain * lax.rsqrt(spread + EPSILON)
    out_ref[...] = leaky(scale * (third_ref[...] - mean) + bias).astype(jnp.bfloat16)


def neighbour(value, by):
    count = lax.axis_size("space")
    return lax.ppermute(value, "space", [(i, (i + by) % count) for i in range(count)])


def exchange(copies, axis):
    return lax.all_to_all(copies, axis, 0, 0, tiled=True)


def struct(shape, dtype=jnp.float32):
    return jax.ShapeDtypeStruct(shape, dtype)


def local(
    features,
    first_weight,
    first_gain,
    first_bias,
    down_weight,
    down_gain,
    down_bias,
    third_weight,
    third_gain,
    third_bias,
):
    spaces, chans = lax.axis_size("space"), lax.axis_size("chan")
    in_chans = features.shape[0]
    n = first_weight.shape[1]
    m = third_weight.shape[1]
    wide = down_weight.shape[1]
    packed_rows = wide * HALF_CELLS // LANES
    first_weight = first_weight.reshape(27 * n, in_chans)
    down_weight = jnp.transpose(down_weight, (0, 2, 1)).reshape(27 * n, wide)
    gains = [v.reshape(1, -1) for v in (first_gain, down_gain, third_gain)]
    biases = [v.reshape(1, -1) for v in (first_bias, down_bias, third_bias)]
    unit = 2 * 9 * n * in_chans * CELLS

    slices, send = kernel_call(
        send_kernel,
        (struct((2, in_chans, CELLS), jnp.bfloat16), struct((2, n, CELLS))),
        (features, first_weight),
        4 * unit,
        "send",
    )
    got = neighbour(send, 1)
    own, select, stacked, affine = kernel_call(
        own_kernel,
        (
            struct((2, n, CELLS)),
            struct((9 * HALF_CELLS, CELLS), jnp.bfloat16),
            struct((9, PAIR, 3 * 3 * LANES), jnp.bfloat16),
            struct((AFFINE_ROWS, LANES), jnp.bfloat16),
        ),
        (slices, first_weight, third_weight, gains[1], biases[1]),
        4 * unit,
        "own",
    )
    first0, first1, copies = kernel_call(
        total_kernel,
        (struct((n, CELLS)), struct((n, CELLS)), struct((spaces, LANES))),
        (own, got),
        1 << 20,
        "total",
    )
    first2 = neighbour(first0, -1)
    rows = exchange(copies, "space")
    copies = kernel_call(
        down_kernel,
        struct((chans, packed_rows + AFFINE_ROWS, LANES), jnp.bfloat16),
        (rows, first0, first1, first2, gains[0], biases[0], select, down_weight, affine),
        unit,
        "down",
    )
    parts = exchange(copies, "chan")
    packed, affine, copies = kernel_call(
        reduced_kernel,
        (struct((packed_rows, LANES)), struct((AFFINE_ROWS, LANES)), struct((spaces, 5 * LANES))),
        (parts,),
        1 << 20,
        "reduced",
    )
    before, after = neighbour(packed, 1), neighbour(packed, -1)
    rows = exchange(copies, "space")
    third, copies = kernel_call(
        third_kernel,
        (struct((m, HALF_CELLS)), struct((spaces, LANES))),
        (rows, packed, before, after, affine, stacked),
        unit,
        "third",
    )
    rows = exchange(copies, "space")
    out = kernel_call(
        last_kernel,
        struct((m, HALF_CELLS), jnp.bfloat16),
        (rows, third, gains[2], biases[2]),
        1 << 20,
        "last",
    )
    return out.reshape(m, 1, HALF_CELLS)


def solution(mesh):
    return jax.shard_map(
        local,
        mesh=mesh,
        in_specs=(
            P(None, "space", None),
            P(None, "chan", None),
            P("chan"),
            P("chan"),
            P(None, None, "chan"),
            P("chan"),
            P("chan"),
            P(None, "chan", None),
            P("chan"),
            P("chan"),
        ),
        out_specs=P("chan", "space", None),
        check_vma=False,
    )
```

```python
import jax
import jax.numpy as jnp
from jax import lax
from jax.experimental import pallas as pl
from jax.experimental.pallas import tpu as pltpu
from jax.sharding import PartitionSpec as P

ROWS = 16
COLS = 32
CELLS = ROWS * COLS
HALF_ROWS = ROWS // 2
HALF_COLS = COLS // 2
HALF_CELLS = HALF_ROWS * HALF_COLS
LANES = 128
PAIR = 48
EPSILON = 1e-05
SLOPE = 0.01

VMEM = pl.BlockSpec(memory_space=pltpu.VMEM)
HBM = pl.BlockSpec(memory_space=pltpu.HBM)


def kernel_call(body, outputs, operands, flops, name, in_specs=None, scratch=()):
    return pl.pallas_call(
        body,
        out_shape=outputs,
        in_specs=in_specs or [VMEM] * len(operands),
        out_specs=jax.tree.map(lambda _: VMEM, outputs),
        scratch_shapes=scratch,
        compiler_params=pltpu.CompilerParams(vmem_limit_bytes=32 * 1024 * 1024),
        cost_estimate=pl.CostEstimate(flops=flops, bytes_accessed=2 << 20, transcendentals=0),
        name=name,
    )(*operands)


def iota(shape, dim):
    return lax.broadcasted_iota(jnp.int32, shape, dim)


def dot(a, b):
    return jnp.dot(a, b, preferred_element_type=jnp.float32)


def dot_nt(a, b):
    return lax.dot_general(a, b, (((1,), (1,)), ((), ())), preferred_element_type=jnp.float32)


def to_row(column, offset):
    n = column.shape[0]
    hit = iota((n, LANES), 1) == iota((n, LANES), 0) + offset
    return jnp.sum(jnp.where(hit, column, 0.0), axis=0, keepdims=True)


def to_column(row, offset, n):
    width = row.shape[1]
    hit = iota((n, width), 1) == iota((n, width), 0) + offset
    return jnp.sum(jnp.where(hit, row, 0.0), axis=1, keepdims=True)


def shift_add(taps, out_chans, row_count, col_count):
    cells = row_count * col_count
    block = 3 * out_chans
    cell = iota((block, cells), 1)
    above = pltpu.roll(taps[:block], col_count, axis=1)
    below = pltpu.roll(taps[2 * block :], cells - col_count, axis=1)
    rows = (
        taps[block : 2 * block]
        + jnp.where(cell >= col_count, above, 0.0)
        + jnp.where(cell < cells - col_count, below, 0.0)
    )
    column = iota((out_chans, cells), 1) % col_count
    left = pltpu.roll(rows[:out_chans], 1, axis=1)
    right = pltpu.roll(rows[2 * out_chans :], cells - 1, axis=1)
    return (
        rows[out_chans : 2 * out_chans]
        + jnp.where(column != 0, left, 0.0)
        + jnp.where(column != col_count - 1, right, 0.0)
    )


def leaky(value):
    return jnp.where(value >= 0, value, SLOPE * value)


def send_kernel(
    features_hbm, weight_hbm, slices_ref, up_ref, down_ref, features_ref, weight_ref, sems
):
    loads = [
        pltpu.make_async_copy(features_hbm, features_ref, sems.at[0]),
        pltpu.make_async_copy(weight_hbm, weight_ref, sems.at[1]),
    ]
    for load in loads:
        load.start()
    chans = features_ref.shape[0]
    loads[0].wait()
    pairs = features_ref[...].reshape(2 * chans, CELLS)
    for j in range(2):
        pick = (iota((chans, 2 * chans), 1) == 2 * iota((chans, 2 * chans), 0) + j).astype(
            jnp.bfloat16
        )
        slices_ref[j] = dot(pick, pairs).astype(jnp.bfloat16)
    block = weight_ref.shape[0] // 3
    out_chans = block // 9
    lower, upper = slices_ref[0], slices_ref[1]
    loads[1].wait()
    tap0, tap1, tap2 = (weight_ref[k * block : (k + 1) * block] for k in range(3))
    up_ref[0] = shift_add(dot(tap0, lower) + dot(tap1, upper), out_chans, ROWS, COLS)
    up_ref[1] = shift_add(dot(tap0, upper), out_chans, ROWS, COLS)
    at_start = lax.axis_index("space") == 0
    down_ref[...] = jnp.where(at_start, 0.0, shift_add(dot(tap2, lower), out_chans, ROWS, COLS))


def own_kernel(slices_ref, weight_ref, third_ref, own_ref, select_ref, stacked_ref):
    block = weight_ref.shape[0] // 3
    out_chans = block // 9
    lower, upper = slices_ref[0], slices_ref[1]
    tap1, tap2 = weight_ref[block : 2 * block], weight_ref[2 * block :]
    own_ref[...] = shift_add(dot(tap1, lower) + dot(tap2, upper), out_chans, ROWS, COLS)

    place = iota((HALF_CELLS, CELLS), 0)
    cell = iota((HALF_CELLS, CELLS), 1)
    row, column = cell // COLS, cell % COLS
    row_gap = row - 2 * (place // HALF_COLS)
    column_gap = column - 2 * (place % HALF_COLS)
    for tap in range(9):
        hit = (row_gap == tap // 3 - 1) & (column_gap == tap % 3 - 1)
        select_ref[tap * HALF_CELLS : (tap + 1) * HALF_CELLS] = hit.astype(jnp.bfloat16)

    third_out, third_in = third_ref.shape[1:]
    stacked_ref[...] = jnp.zeros_like(stacked_ref)
    wide = stacked_ref.shape[2] // 3
    for depth in range(3):
        for tap in range(9):
            stacked_ref[tap, :third_out, depth * wide : depth * wide + third_in] = third_ref[
                depth * 9 + tap
            ]


def total_kernel(up_ref, down_ref, own_ref, got_ref, back_ref, first_ref, copies_ref):
    at_start = lax.axis_index("space") == 0
    first0 = got_ref[0] + down_ref[...]
    first1 = own_ref[...] + jnp.where(at_start, 0.0, got_ref[1])
    first_ref[0] = first0
    first_ref[1] = first1
    first_ref[2] = up_ref[0] + back_ref[...]
    cells = 2 * CELLS
    mean = (
        jnp.sum(first0, axis=1, keepdims=True) + jnp.sum(first1, axis=1, keepdims=True)
    ) / cells
    spread = (
        jnp.sum((first0 - mean) ** 2, axis=1, keepdims=True)
        + jnp.sum((first1 - mean) ** 2, axis=1, keepdims=True)
    ) / cells
    row = to_row(mean, 0) + to_row(spread, mean.shape[0])
    copies_ref[...] = jnp.broadcast_to(row, copies_ref.shape)


def column_statistics(rows, n):
    average = jnp.mean(rows, axis=0, keepdims=True)
    apart = jnp.mean((rows - average) ** 2, axis=0, keepdims=True)
    mean = to_column(average, 0, n)
    spread = to_column(average, n, n) + to_column(apart, 0, n)
    return mean, spread


def down_kernel(
    rows_ref, first_ref, gain_ref, bias_ref, select_ref, weight_ref, parts_ref
):
    n = first_ref.shape[1]
    mean, spread = column_statistics(rows_ref[...], n)
    gain = to_column(gain_ref[...], 0, n)
    bias = to_column(bias_ref[...], 0, n)
    scale = gain * lax.rsqrt(spread + EPSILON)
    at_start = lax.axis_index("space") == 0
    levels = [leaky(scale * (first_ref[k] - mean) + bias) for k in range(3)]
    levels[0] = jnp.where(at_start, 0.0, levels[0])
    levels.append(jnp.zeros((LANES - 3 * n, CELLS), jnp.float32))
    layers = jnp.concatenate(levels, axis=0).astype(jnp.bfloat16)
    out_chans = weight_ref.shape[1]
    picked = dot_nt(select_ref[...], layers).astype(jnp.bfloat16)
    windows, weights = [], []
    for tap in range(9):
        windows.append(picked[tap * HALF_CELLS : (tap + 1) * HALF_CELLS])
        for depth in range(3):
            at = (depth * 9 + tap) * n
            weights.append(weight_ref[at : at + n])
        weights.append(jnp.zeros((LANES - 3 * n, out_chans), jnp.bfloat16))
    parts = dot(jnp.concatenate(windows, axis=1), jnp.concatenate(weights, axis=0))
    spare = -out_chans % LANES
    parts = jnp.concatenate([parts, jnp.zeros((HALF_CELLS, spare), jnp.float32)], axis=1).T
    share = parts_ref.shape[1]
    for c in range(parts_ref.shape[0]):
        parts_ref[c] = parts[c * share : (c + 1) * share].astype(jnp.bfloat16)


def own_statistics(value):
    cells = value.shape[1]
    mean = jnp.sum(value, axis=1, keepdims=True) / cells
    spread = jnp.sum((value - mean) ** 2, axis=1, keepdims=True) / cells
    return to_row(mean, 0) + to_row(spread, value.shape[0])


def reduced_kernel(parts_ref, reduced_ref, copies_ref):
    total = parts_ref[0].astype(jnp.float32)
    for c in range(1, parts_ref.shape[0]):
        total = total + parts_ref[c].astype(jnp.float32)
    reduced_ref[...] = total
    copies_ref[...] = jnp.broadcast_to(own_statistics(total), copies_ref.shape)


def bottom_kernel(rows_ref, before_ref, own_ref, after_ref, gain_ref, bias_ref, copies_ref):
    n = own_ref.shape[0]
    mean, spread = column_statistics(rows_ref[...], n)
    gain = to_column(gain_ref[...], 0, n)
    bias = to_column(bias_ref[...], 0, n)
    scale = gain * lax.rsqrt(spread + EPSILON)
    space = lax.axis_index("space")
    keeps = (space != 0, None, space != lax.axis_size("space") - 1)
    for k, (ref, keep) in enumerate(zip((before_ref, own_ref, after_ref), keeps)):
        bottom = leaky(scale * (ref[...] - mean) + bias)
        if keep is not None:
            bottom = jnp.where(keep, bottom, 0.0)
        bottom = bottom.astype(jnp.bfloat16)
        for c in range(copies_ref.shape[0]):
            copies_ref[c, k] = bottom


def third_kernel(bottom_ref, stacked_ref, third_ref, copies_ref):
    chans, depths, share, cells = bottom_ref.shape
    wide = stacked_ref.shape[2] // depths
    blocks = []
    for k in range(depths):
        blocks += [bottom_ref[c, k].astype(jnp.float32) for c in range(chans)]
        blocks.append(jnp.zeros((wide - chans * share, cells), jnp.float32))
    bottom = jnp.concatenate(blocks, axis=0).astype(jnp.bfloat16)
    taps = dot(stacked_ref[...].reshape(9 * PAIR, bottom.shape[0]), bottom)
    third = shift_add(taps, PAIR, HALF_ROWS, HALF_COLS)[: third_ref.shape[0]]
    third_ref[...] = third
    copies_ref[...] = jnp.broadcast_to(own_statistics(third), copies_ref.shape)


def last_kernel(rows_ref, third_ref, gain_ref, bias_ref, out_ref):
    n = third_ref.shape[0]
    mean, spread = column_statistics(rows_ref[...], n)
    gain = to_column(gain_ref[...], 0, n)
    bias = to_column(bias_ref[...], 0, n)
    scale = gain * lax.rsqrt(spread + EPSILON)
    out_ref[...] = leaky(scale * (third_ref[...] - mean) + bias).astype(jnp.bfloat16)


def neighbour(value, by):
    count = lax.axis_size("space")
    return lax.ppermute(value, "space", [(i, (i + by) % count) for i in range(count)])


def exchange(copies, axis):
    return lax.all_to_all(copies, axis, 0, 0, tiled=True)


def struct(shape, dtype=jnp.float32):
    return jax.ShapeDtypeStruct(shape, dtype)


def local(
    features,
    first_weight,
    first_gain,
    first_bias,
    down_weight,
    down_gain,
    down_bias,
    third_weight,
    third_gain,
    third_bias,
):
    spaces, chans = lax.axis_size("space"), lax.axis_size("chan")
    in_chans = features.shape[0]
    n = first_weight.shape[1]
    m = third_weight.shape[1]
    wide = down_weight.shape[1]
    first_weight = first_weight.reshape(27 * n, in_chans)
    down_weight = jnp.transpose(down_weight, (0, 2, 1)).reshape(27 * n, wide)
    gains = [v.reshape(1, -1) for v in (first_gain, down_gain, third_gain)]
    biases = [v.reshape(1, -1) for v in (first_bias, down_bias, third_bias)]
    unit = 2 * 9 * n * in_chans * CELLS

    slices, up, down = kernel_call(
        send_kernel,
        (
            struct((2, in_chans, CELLS), jnp.bfloat16),
            struct((2, n, CELLS)),
            struct((n, CELLS)),
        ),
        (features, first_weight),
        4 * unit,
        "send",
        in_specs=[HBM, HBM],
        scratch=[
            pltpu.VMEM(features.shape, jnp.bfloat16),
            pltpu.VMEM(first_weight.shape, jnp.bfloat16),
            pltpu.SemaphoreType.DMA((2,)),
        ],
    )
    got = neighbour(up, 1)
    back = neighbour(down, -1)
    own, select, stacked = kernel_call(
        own_kernel,
        (
            struct((n, CELLS)),
            struct((9 * HALF_CELLS, CELLS), jnp.bfloat16),
            struct((9, PAIR, 3 * 3 * LANES), jnp.bfloat16),
        ),
        (slices, first_weight, third_weight),
        2 * unit,
        "own",
    )
    first, copies = kernel_call(
        total_kernel,
        (struct((3, n, CELLS)), struct((spaces, LANES))),
        (up, down, own, got, back),
        1 << 20,
        "total",
    )
    rows = exchange(copies, "space")
    parts = kernel_call(
        down_kernel,
        struct((chans, m, HALF_CELLS), jnp.bfloat16),
        (rows, first, gains[0], biases[0], select, down_weight),
        unit,
        "down",
    )
    parts = exchange(parts, "chan")
    reduced, copies = kernel_call(
        reduced_kernel,
        (struct((m, HALF_CELLS)), struct((spaces, LANES))),
        (parts,),
        1 << 20,
        "reduced",
    )
    before, after = neighbour(reduced, 1), neighbour(reduced, -1)
    rows = exchange(copies, "space")
    copies = kernel_call(
        bottom_kernel,
        struct((chans, 3, m, HALF_CELLS), jnp.bfloat16),
        (rows, before, reduced, after, gains[1], biases[1]),
        1 << 20,
        "bottom",
    )
    bottom = exchange(copies, "chan")
    third, copies = kernel_call(
        third_kernel,
        (struct((m, HALF_CELLS)), struct((spaces, LANES))),
        (bottom, stacked),
        unit,
        "third",
    )
    rows = exchange(copies, "space")
    out = kernel_call(
        last_kernel,
        struct((m, HALF_CELLS), jnp.bfloat16),
        (rows, third, gains[2], biases[2]),
        1 << 20,
        "last",
    )
    return out.reshape(m, 1, HALF_CELLS)


def solution(mesh):
    return jax.shard_map(
        local,
        mesh=mesh,
        in_specs=(
            P(None, "space", None),
            P(None, "chan", None),
            P("chan"),
            P("chan"),
            P(None, None, "chan"),
            P("chan"),
            P("chan"),
            P(None, "chan", None),
            P("chan"),
            P("chan"),
        ),
        out_specs=P("chan", "space", None),
        check_vma=False,
    )
```

```python
import jax
import jax.numpy as jnp
from jax import lax
from jax.experimental import pallas as pl
from jax.experimental.pallas import tpu as pltpu
from jax.sharding import PartitionSpec as P

ROWS = 16
COLS = 32
CELLS = ROWS * COLS
HALF_ROWS = ROWS // 2
HALF_COLS = COLS // 2
HALF_CELLS = HALF_ROWS * HALF_COLS
LANES = 128
PAIR = 48
EPSILON = 1e-05
SLOPE = 0.01

VMEM = pl.BlockSpec(memory_space=pltpu.VMEM)
HBM = pl.BlockSpec(memory_space=pltpu.HBM)


def kernel_call(body, outputs, operands, flops, name, in_specs=None, scratch=()):
    return pl.pallas_call(
        body,
        out_shape=outputs,
        in_specs=in_specs or [VMEM] * len(operands),
        out_specs=jax.tree.map(lambda _: VMEM, outputs),
        scratch_shapes=scratch,
        compiler_params=pltpu.CompilerParams(vmem_limit_bytes=32 * 1024 * 1024),
        cost_estimate=pl.CostEstimate(flops=flops, bytes_accessed=2 << 20, transcendentals=0),
        name=name,
    )(*operands)


def iota(shape, dim):
    return lax.broadcasted_iota(jnp.int32, shape, dim)


def dot(a, b):
    return jnp.dot(a, b, preferred_element_type=jnp.float32)


def dot_nt(a, b):
    return lax.dot_general(a, b, (((1,), (1,)), ((), ())), preferred_element_type=jnp.float32)


def to_row(column, offset):
    n = column.shape[0]
    hit = iota((n, LANES), 1) == iota((n, LANES), 0) + offset
    return jnp.sum(jnp.where(hit, column, 0.0), axis=0, keepdims=True)


def to_column(row, offset, n):
    width = row.shape[1]
    hit = iota((n, width), 1) == iota((n, width), 0) + offset
    return jnp.sum(jnp.where(hit, row, 0.0), axis=1, keepdims=True)


def shift_add(taps, out_chans, row_count, col_count):
    cells = row_count * col_count
    block = 3 * out_chans
    cell = iota((block, cells), 1)
    above = pltpu.roll(taps[:block], col_count, axis=1)
    below = pltpu.roll(taps[2 * block :], cells - col_count, axis=1)
    rows = (
        taps[block : 2 * block]
        + jnp.where(cell >= col_count, above, 0.0)
        + jnp.where(cell < cells - col_count, below, 0.0)
    )
    column = iota((out_chans, cells), 1) % col_count
    left = pltpu.roll(rows[:out_chans], 1, axis=1)
    right = pltpu.roll(rows[2 * out_chans :], cells - 1, axis=1)
    return (
        rows[out_chans : 2 * out_chans]
        + jnp.where(column != 0, left, 0.0)
        + jnp.where(column != col_count - 1, right, 0.0)
    )


def leaky(value):
    return jnp.where(value >= 0, value, SLOPE * value)


def send_kernel(
    features_hbm, weight_hbm, slices_ref, cross_ref, pair_ref, features_ref, weight_ref, sems
):
    loads = [
        pltpu.make_async_copy(features_hbm, features_ref, sems.at[0]),
        pltpu.make_async_copy(weight_hbm, weight_ref, sems.at[1]),
    ]
    for load in loads:
        load.start()
    chans = features_ref.shape[0]
    loads[0].wait()
    pairs = features_ref[...].reshape(2 * chans, CELLS)
    for j in range(2):
        pick = (iota((chans, 2 * chans), 1) == 2 * iota((chans, 2 * chans), 0) + j).astype(
            jnp.bfloat16
        )
        slices_ref[j] = dot(pick, pairs).astype(jnp.bfloat16)
    block = weight_ref.shape[0] // 3
    out_chans = block // 9
    lower, upper = slices_ref[0], slices_ref[1]
    loads[1].wait()
    tap0, tap1, tap2 = (weight_ref[k * block : (k + 1) * block] for k in range(3))
    up0 = shift_add(dot(tap0, lower) + dot(tap1, upper), out_chans, ROWS, COLS)
    up1 = shift_add(dot(tap0, upper), out_chans, ROWS, COLS)
    down = jnp.where(slab() == 0, 0.0, shift_add(dot(tap2, lower), out_chans, ROWS, COLS))
    even = lax.axis_index("core") == 0
    cross_ref[0] = jnp.where(even, down, up0)
    cross_ref[1] = up1
    pair_ref[0] = jnp.where(even, up0, down)
    pair_ref[1] = up1


def own_kernel(slices_ref, weight_ref, third_ref, own_ref, select_ref, stacked_ref):
    block = weight_ref.shape[0] // 3
    out_chans = block // 9
    lower, upper = slices_ref[0], slices_ref[1]
    tap1, tap2 = weight_ref[block : 2 * block], weight_ref[2 * block :]
    own_ref[...] = shift_add(dot(tap1, lower) + dot(tap2, upper), out_chans, ROWS, COLS)

    place = iota((HALF_CELLS, CELLS), 0)
    cell = iota((HALF_CELLS, CELLS), 1)
    row, column = cell // COLS, cell % COLS
    row_gap = row - 2 * (place // HALF_COLS)
    column_gap = column - 2 * (place % HALF_COLS)
    for tap in range(9):
        hit = (row_gap == tap // 3 - 1) & (column_gap == tap % 3 - 1)
        select_ref[tap * HALF_CELLS : (tap + 1) * HALF_CELLS] = hit.astype(jnp.bfloat16)

    third_out, third_in = third_ref.shape[1:]
    stacked_ref[...] = jnp.zeros_like(stacked_ref)
    wide = stacked_ref.shape[2] // 3
    for depth in range(3):
        for tap in range(9):
            stacked_ref[tap, :third_out, depth * wide : depth * wide + third_in] = third_ref[
                depth * 9 + tap
            ]


def total_kernel(cross_ref, pair_ref, own_ref, got_cross_ref, got_pair_ref, first_ref, copies_ref):
    even = lax.axis_index("core") == 0

    def choose(if_even, if_odd):
        return jnp.where(even, if_even, if_odd)

    first0 = choose(cross_ref[0], pair_ref[0]) + choose(got_cross_ref[0], got_pair_ref[0])
    first1 = own_ref[...] + jnp.where(
        slab() == 0, 0.0, choose(got_cross_ref[1], got_pair_ref[1])
    )
    first_ref[0] = first0
    first_ref[1] = first1
    first_ref[2] = choose(pair_ref[0], cross_ref[0]) + choose(got_pair_ref[0], got_cross_ref[0])
    cells = 2 * CELLS
    mean = (
        jnp.sum(first0, axis=1, keepdims=True) + jnp.sum(first1, axis=1, keepdims=True)
    ) / cells
    spread = (
        jnp.sum((first0 - mean) ** 2, axis=1, keepdims=True)
        + jnp.sum((first1 - mean) ** 2, axis=1, keepdims=True)
    ) / cells
    row = to_row(mean, 0) + to_row(spread, mean.shape[0])
    copies_ref[...] = jnp.broadcast_to(row, copies_ref.shape)


def column_statistics(rows, n):
    average = jnp.mean(rows, axis=0, keepdims=True)
    apart = jnp.mean((rows - average) ** 2, axis=0, keepdims=True)
    mean = to_column(average, 0, n)
    spread = to_column(average, n, n) + to_column(apart, 0, n)
    return mean, spread


def down_kernel(
    rows_ref, first_ref, gain_ref, bias_ref, select_ref, weight_ref, parts_ref
):
    n = first_ref.shape[1]
    mean, spread = column_statistics(rows_ref[...], n)
    gain = to_column(gain_ref[...], 0, n)
    bias = to_column(bias_ref[...], 0, n)
    scale = gain * lax.rsqrt(spread + EPSILON)
    levels = [leaky(scale * (first_ref[k] - mean) + bias) for k in range(3)]
    levels[0] = jnp.where(slab() == 0, 0.0, levels[0])
    levels.append(jnp.zeros((LANES - 3 * n, CELLS), jnp.float32))
    layers = jnp.concatenate(levels, axis=0).astype(jnp.bfloat16)
    out_chans = weight_ref.shape[1]
    picked = dot_nt(select_ref[...], layers).astype(jnp.bfloat16)
    windows, weights = [], []
    for tap in range(9):
        windows.append(picked[tap * HALF_CELLS : (tap + 1) * HALF_CELLS])
        for depth in range(3):
            at = (depth * 9 + tap) * n
            weights.append(weight_ref[at : at + n])
        weights.append(jnp.zeros((LANES - 3 * n, out_chans), jnp.bfloat16))
    parts = dot(jnp.concatenate(windows, axis=1), jnp.concatenate(weights, axis=0))
    spare = -out_chans % LANES
    parts = jnp.concatenate([parts, jnp.zeros((HALF_CELLS, spare), jnp.float32)], axis=1).T
    share = parts_ref.shape[1]
    chans = out_chans // share
    for c in range(chans):
        part = parts[c * share : (c + 1) * share].astype(jnp.bfloat16)
        for core in range(2):
            parts_ref[core * chans + c] = part


def own_statistics(value):
    cells = value.shape[1]
    mean = jnp.sum(value, axis=1, keepdims=True) / cells
    spread = jnp.sum((value - mean) ** 2, axis=1, keepdims=True) / cells
    return to_row(mean, 0) + to_row(spread, value.shape[0])


def reduced_kernel(parts_ref, reduced_ref, mine_ref, copies_ref):
    chans = parts_ref.shape[0] // 2
    totals = []
    for core in range(2):
        total = parts_ref[core * chans].astype(jnp.float32)
        for c in range(1, chans):
            total = total + parts_ref[core * chans + c].astype(jnp.float32)
        reduced_ref[core] = total
        totals.append(total)
    mine_ref[...] = jnp.where(lax.axis_index("core") == 0, totals[0], totals[1])
    row = own_statistics(jnp.concatenate(totals, axis=1))
    copies_ref[...] = jnp.broadcast_to(row, copies_ref.shape)


def bottom_kernel(rows_ref, reduced_ref, got_ref, gain_ref, bias_ref, copies_ref):
    n = got_ref.shape[0]
    mean, spread = column_statistics(rows_ref[...], n)
    gain = to_column(gain_ref[...], 0, n)
    bias = to_column(bias_ref[...], 0, n)
    scale = gain * lax.rsqrt(spread + EPSILON)
    even = lax.axis_index("core") == 0
    space = slab()
    last = 2 * lax.axis_size("chip") - 1
    got, reduced0, reduced1 = got_ref[...], reduced_ref[0], reduced_ref[1]
    slices = (
        (jnp.where(even, got, reduced0), space != 0),
        (jnp.where(even, reduced0, reduced1), None),
        (jnp.where(even, reduced1, got), space != last),
    )
    for k, (value, keep) in enumerate(slices):
        bottom = leaky(scale * (value - mean) + bias)
        if keep is not None:
            bottom = jnp.where(keep, bottom, 0.0)
        bottom = bottom.astype(jnp.bfloat16)
        for c in range(copies_ref.shape[0]):
            copies_ref[c, k] = bottom


def third_kernel(bottom_ref, stacked_ref, third_ref, copies_ref):
    chans, depths, share, cells = bottom_ref.shape
    wide = stacked_ref.shape[2] // depths
    blocks = []
    for k in range(depths):
        blocks += [bottom_ref[c, k].astype(jnp.float32) for c in range(chans)]
        blocks.append(jnp.zeros((wide - chans * share, cells), jnp.float32))
    bottom = jnp.concatenate(blocks, axis=0).astype(jnp.bfloat16)
    taps = dot(stacked_ref[...].reshape(9 * PAIR, bottom.shape[0]), bottom)
    third = shift_add(taps, PAIR, HALF_ROWS, HALF_COLS)[: third_ref.shape[0]]
    third_ref[...] = third
    copies_ref[...] = jnp.broadcast_to(own_statistics(third), copies_ref.shape)


def last_kernel(rows_ref, third_ref, gain_ref, bias_ref, out_ref):
    n = third_ref.shape[0]
    mean, spread = column_statistics(rows_ref[...], n)
    gain = to_column(gain_ref[...], 0, n)
    bias = to_column(bias_ref[...], 0, n)
    scale = gain * lax.rsqrt(spread + EPSILON)
    out_ref[...] = leaky(scale * (third_ref[...] - mean) + bias).astype(jnp.bfloat16)


def slab():
    return 2 * lax.axis_index("chip") + lax.axis_index("core")


def across(value):
    count = 2 * lax.axis_size("chip")
    pairs = [(i, (i + 2 * (i % 2) - 1) % count) for i in range(count)]
    return lax.ppermute(value, ("chip", "core"), pairs)


def beside(value):
    return lax.ppermute(value, "core", [(0, 1), (1, 0)])


def exchange(copies, axes):
    return lax.all_to_all(copies, axes, 0, 0, tiled=True)


def struct(shape, dtype=jnp.float32):
    return jax.ShapeDtypeStruct(shape, dtype)


def local(
    features,
    first_weight,
    first_gain,
    first_bias,
    down_weight,
    down_gain,
    down_bias,
    third_weight,
    third_gain,
    third_bias,
):
    chips, chans = lax.axis_size("chip"), lax.axis_size("chan")
    in_chans = features.shape[0]
    n = first_weight.shape[1]
    m = third_weight.shape[1]
    wide = down_weight.shape[1]
    first_weight = first_weight.reshape(27 * n, in_chans)
    down_weight = jnp.transpose(down_weight, (0, 2, 1)).reshape(27 * n, wide)
    gains = [v.reshape(1, -1) for v in (first_gain, down_gain, third_gain)]
    biases = [v.reshape(1, -1) for v in (first_bias, down_bias, third_bias)]
    unit = 2 * 9 * n * in_chans * CELLS

    slices, cross, pair = kernel_call(
        send_kernel,
        (
            struct((2, in_chans, CELLS), jnp.bfloat16),
            struct((2, n, CELLS)),
            struct((2, n, CELLS)),
        ),
        (
            pltpu.with_memory_space_constraint(features, pltpu.HBM),
            pltpu.with_memory_space_constraint(first_weight, pltpu.HBM),
        ),
        4 * unit,
        "send",
        in_specs=[HBM, HBM],
        scratch=[
            pltpu.VMEM(features.shape, jnp.bfloat16),
            pltpu.VMEM(first_weight.shape, jnp.bfloat16),
            pltpu.SemaphoreType.DMA((2,)),
        ],
    )
    got_cross, got_pair = across(cross), beside(pair)
    own, select, stacked = kernel_call(
        own_kernel,
        (
            struct((n, CELLS)),
            struct((9 * HALF_CELLS, CELLS), jnp.bfloat16),
            struct((9, PAIR, 3 * 3 * LANES), jnp.bfloat16),
        ),
        (slices, first_weight, third_weight),
        2 * unit,
        "own",
    )
    first, copies = kernel_call(
        total_kernel,
        (struct((3, n, CELLS)), struct((2 * chips, LANES))),
        (cross, pair, own, got_cross, got_pair),
        1 << 20,
        "total",
    )
    rows = exchange(copies, ("chip", "core"))
    parts = kernel_call(
        down_kernel,
        struct((2 * chans, m, HALF_CELLS), jnp.bfloat16),
        (rows, first, gains[0], biases[0], select, down_weight),
        unit,
        "down",
    )
    parts = exchange(parts, ("core", "chan"))
    reduced, mine, copies = kernel_call(
        reduced_kernel,
        (struct((2, m, HALF_CELLS)), struct((m, HALF_CELLS)), struct((chips, LANES))),
        (parts,),
        1 << 20,
        "reduced",
    )
    got = across(mine)
    rows = exchange(copies, "chip")
    copies = kernel_call(
        bottom_kernel,
        struct((chans, 3, m, HALF_CELLS), jnp.bfloat16),
        (rows, reduced, got, gains[1], biases[1]),
        1 << 20,
        "bottom",
    )
    bottom = exchange(copies, "chan")
    third, copies = kernel_call(
        third_kernel,
        (struct((m, HALF_CELLS)), struct((2 * chips, LANES))),
        (bottom, stacked),
        unit,
        "third",
    )
    rows = exchange(copies, ("chip", "core"))
    out = kernel_call(
        last_kernel,
        struct((m, HALF_CELLS), jnp.bfloat16),
        (rows, third, gains[2], biases[2]),
        1 << 20,
        "last",
    )
    return out.reshape(m, 1, HALF_CELLS)


def solution(mesh):
    chans = mesh.shape["chan"]
    pairs = jax.sharding.Mesh(mesh.devices.reshape(-1, 2, chans), ("chip", "core", "chan"))
    space = ("chip", "core")
    return jax.shard_map(
        local,
        mesh=pairs,
        in_specs=(
            P(None, space, None),
            P(None, "chan", None),
            P("chan"),
            P("chan"),
            P(None, None, "chan"),
            P("chan"),
            P("chan"),
            P(None, "chan", None),
            P("chan"),
            P("chan"),
        ),
        out_specs=P("chan", space, None),
        check_vma=False,
    )
```

```python
import jax
import jax.numpy as jnp
from jax import lax
from jax.experimental import pallas as pl
from jax.experimental.pallas import tpu as pltpu
from jax.sharding import PartitionSpec as P

ROWS = 16
COLS = 32
CELLS = ROWS * COLS
HALF_ROWS = ROWS // 2
HALF_COLS = COLS // 2
HALF_CELLS = HALF_ROWS * HALF_COLS
LANES = 128
PAIR = 48
FIRST_CHIP = 31
SECOND_CHIP = 0
THIRD_CHIP = 20
FIRST_CHAN = 4
EPSILON = 1e-05
SLOPE = 0.01

VMEM = pl.BlockSpec(memory_space=pltpu.VMEM)
HBM = pl.BlockSpec(memory_space=pltpu.HBM)


def kernel_call(body, outputs, operands, flops, name, in_specs=None, scratch=()):
    return pl.pallas_call(
        body,
        out_shape=outputs,
        in_specs=in_specs or [VMEM] * len(operands),
        out_specs=jax.tree.map(lambda _: VMEM, outputs),
        scratch_shapes=scratch,
        compiler_params=pltpu.CompilerParams(vmem_limit_bytes=32 * 1024 * 1024),
        cost_estimate=pl.CostEstimate(flops=flops, bytes_accessed=2 << 20, transcendentals=0),
        name=name,
    )(*operands)


def iota(shape, dim):
    return lax.broadcasted_iota(jnp.int32, shape, dim)


def dot(a, b):
    return jnp.dot(a, b, preferred_element_type=jnp.float32)


def dot_nt(a, b):
    return lax.dot_general(a, b, (((1,), (1,)), ((), ())), preferred_element_type=jnp.float32)


def to_row(column, offset):
    n = column.shape[0]
    hit = iota((n, LANES), 1) == iota((n, LANES), 0) + offset
    return jnp.sum(jnp.where(hit, column, 0.0), axis=0, keepdims=True)


def to_column(row, offset, n):
    width = row.shape[1]
    hit = iota((n, width), 1) == iota((n, width), 0) + offset
    return jnp.sum(jnp.where(hit, row, 0.0), axis=1, keepdims=True)


def shift_add(taps, out_chans, row_count, col_count):
    cells = row_count * col_count
    block = 3 * out_chans
    cell = iota((block, cells), 1)
    above = pltpu.roll(taps[:block], col_count, axis=1)
    below = pltpu.roll(taps[2 * block :], cells - col_count, axis=1)
    rows = (
        taps[block : 2 * block]
        + jnp.where(cell >= col_count, above, 0.0)
        + jnp.where(cell < cells - col_count, below, 0.0)
    )
    column = iota((out_chans, cells), 1) % col_count
    left = pltpu.roll(rows[:out_chans], 1, axis=1)
    right = pltpu.roll(rows[2 * out_chans :], cells - 1, axis=1)
    return (
        rows[out_chans : 2 * out_chans]
        + jnp.where(column != 0, left, 0.0)
        + jnp.where(column != col_count - 1, right, 0.0)
    )


def leaky(value):
    return jnp.where(value >= 0, value, SLOPE * value)


def send_kernel(
    features_hbm, weight_hbm,
    slices_ref, weight_ref, kept_ref, cross_ref, pair_ref,
    features_ref, sems,
):
    loads = [
        pltpu.make_async_copy(features_hbm, features_ref, sems.at[0]),
        pltpu.make_async_copy(weight_hbm, weight_ref, sems.at[1]),
    ]
    for load in loads:
        load.start()
    chans = features_ref.shape[0]
    loads[0].wait()
    pairs = features_ref[...].reshape(2 * chans, CELLS)
    for j in range(2):
        pick = (iota((chans, 2 * chans), 1) == 2 * iota((chans, 2 * chans), 0) + j).astype(
            jnp.bfloat16
        )
        slices_ref[j] = dot(pick, pairs).astype(jnp.bfloat16)
    block = weight_ref.shape[0] // 3
    out_chans = block // 9
    lower, upper = slices_ref[0], slices_ref[1]
    loads[1].wait()
    tap0, tap1, tap2 = (weight_ref[k * block : (k + 1) * block] for k in range(3))
    up0 = shift_add(dot(tap0, lower) + dot(tap1, upper), out_chans, ROWS, COLS)
    up1 = shift_add(dot(tap0, upper), out_chans, ROWS, COLS)
    down = jnp.where(slab() == 0, 0.0, shift_add(dot(tap2, lower), out_chans, ROWS, COLS))
    kept_ref[0] = up0
    kept_ref[1] = down
    even = lax.axis_index("core") == 0
    up1 = up1.astype(jnp.bfloat16)
    cross_ref[0] = jnp.where(even, down, up0).astype(jnp.bfloat16)
    cross_ref[1] = up1
    pair_ref[0] = jnp.where(even, up0, down).astype(jnp.bfloat16)
    pair_ref[1] = up1


def own_kernel(slices_ref, weight_ref, third_ref, own_ref, select_ref, stacked_ref):
    block = weight_ref.shape[0] // 3
    out_chans = block // 9
    lower, upper = slices_ref[0], slices_ref[1]
    tap1, tap2 = weight_ref[block : 2 * block], weight_ref[2 * block :]
    own_ref[...] = shift_add(dot(tap1, lower) + dot(tap2, upper), out_chans, ROWS, COLS)

    place = iota((HALF_CELLS, CELLS), 0)
    cell = iota((HALF_CELLS, CELLS), 1)
    row, column = cell // COLS, cell % COLS
    row_gap = row - 2 * (place // HALF_COLS)
    column_gap = column - 2 * (place % HALF_COLS)
    for tap in range(9):
        hit = (row_gap == tap // 3 - 1) & (column_gap == tap % 3 - 1)
        select_ref[tap * HALF_CELLS : (tap + 1) * HALF_CELLS] = hit.astype(jnp.bfloat16)

    third_out, third_in = third_ref.shape[1:]
    stacked_ref[...] = jnp.zeros_like(stacked_ref)
    wide = stacked_ref.shape[2] // 3
    for depth in range(3):
        for tap in range(9):
            stacked_ref[tap, :third_out, depth * wide : depth * wide + third_in] = third_ref[
                depth * 9 + tap
            ]


def total_kernel(kept_ref, own_ref, got_cross_ref, got_pair_ref, first_ref, copies_ref):
    even = lax.axis_index("core") == 0

    cross = got_cross_ref[...].astype(jnp.float32)
    pair = got_pair_ref[...].astype(jnp.float32)
    first0 = kept_ref[1] + jnp.where(even, cross[0], pair[0])
    first1 = own_ref[...] + jnp.where(slab() == 0, 0.0, jnp.where(even, cross[1], pair[1]))
    first_ref[0] = first0
    first_ref[1] = first1
    first_ref[2] = kept_ref[0] + jnp.where(even, pair[0], cross[0])
    cells = 2 * CELLS
    mean = (
        jnp.sum(first0, axis=1, keepdims=True) + jnp.sum(first1, axis=1, keepdims=True)
    ) / cells
    spread = (
        jnp.sum((first0 - mean) ** 2, axis=1, keepdims=True)
        + jnp.sum((first1 - mean) ** 2, axis=1, keepdims=True)
    ) / cells
    row = to_row(mean, 0) + to_row(spread, mean.shape[0])
    copies_ref[...] = jnp.broadcast_to(row, copies_ref.shape)


def column_statistics(rows, n):
    average = jnp.mean(rows, axis=0, keepdims=True)
    apart = jnp.mean((rows - average) ** 2, axis=0, keepdims=True)
    mean = to_column(average, 0, n)
    spread = to_column(average, n, n) + to_column(apart, 0, n)
    return mean, spread


def down_kernel(
    rows_ref, first_ref, gain_ref, bias_ref, select_ref, weight_ref, parts_ref
):
    n = first_ref.shape[1]
    mean, spread = column_statistics(rows_ref[...], n)
    gain = to_column(gain_ref[...], 0, n)
    bias = to_column(bias_ref[...], 0, n)
    scale = gain * lax.rsqrt(spread + EPSILON)
    levels = [leaky(scale * (first_ref[k] - mean) + bias) for k in range(3)]
    levels[0] = jnp.where(slab() == 0, 0.0, levels[0])
    levels.append(jnp.zeros((LANES - 3 * n, CELLS), jnp.float32))
    layers = jnp.concatenate(levels, axis=0).astype(jnp.bfloat16)
    out_chans = weight_ref.shape[1]
    picked = dot_nt(select_ref[...], layers).astype(jnp.bfloat16)
    windows, weights = [], []
    for tap in range(9):
        windows.append(picked[tap * HALF_CELLS : (tap + 1) * HALF_CELLS])
        for depth in range(3):
            at = (depth * 9 + tap) * n
            weights.append(weight_ref[at : at + n])
        weights.append(jnp.zeros((LANES - 3 * n, out_chans), jnp.bfloat16))
    parts = dot(jnp.concatenate(windows, axis=1), jnp.concatenate(weights, axis=0))
    spare = -out_chans % LANES
    parts = jnp.concatenate([parts, jnp.zeros((HALF_CELLS, spare), jnp.float32)], axis=1).T
    chans = lax.axis_size("chan")
    share = out_chans // chans
    parts = jnp.concatenate(
        [parts[c * share : (c + 1) * share] for c in turned(chans, FIRST_CHAN)], axis=0
    ).astype(jnp.bfloat16)
    for core in range(2):
        parts_ref[core * out_chans : (core + 1) * out_chans] = parts


def own_statistics(value):
    cells = value.shape[1]
    mean = jnp.sum(value, axis=1, keepdims=True) / cells
    spread = jnp.sum((value - mean) ** 2, axis=1, keepdims=True) / cells
    return to_row(mean, 0) + to_row(spread, value.shape[0])


def reduced_kernel(parts_ref, reduced_ref, mine_ref, copies_ref):
    share = reduced_ref.shape[1]
    parts = parts_ref[...].astype(jnp.float32)
    chans = parts.shape[0] // (2 * share)
    totals = []
    for core in range(2):
        shares = [
            parts[(core * chans + c) * share : (core * chans + c + 1) * share]
            for c in range(chans)
        ]
        totals.append(sum(shares[1:], shares[0]))
        reduced_ref[core] = totals[core]
    mine_ref[...] = jnp.where(lax.axis_index("core") == 0, totals[0], totals[1])
    row = own_statistics(jnp.concatenate(totals, axis=1))
    copies_ref[...] = jnp.broadcast_to(row, copies_ref.shape)


def bottom_kernel(rows_ref, reduced_ref, got_ref, gain_ref, bias_ref, copies_ref):
    n = got_ref.shape[0]
    mean, spread = column_statistics(rows_ref[...], n)
    gain = to_column(gain_ref[...], 0, n)
    bias = to_column(bias_ref[...], 0, n)
    scale = gain * lax.rsqrt(spread + EPSILON)
    even = lax.axis_index("core") == 0
    space = slab()
    last = 2 * lax.axis_size("chip") - 1
    got, reduced0, reduced1 = got_ref[...], reduced_ref[0], reduced_ref[1]
    slices = (
        (jnp.where(even, got, reduced0), space != 0),
        (jnp.where(even, reduced0, reduced1), None),
        (jnp.where(even, reduced1, got), space != last),
    )
    bottoms = []
    for value, keep in slices:
        bottom = leaky(scale * (value - mean) + bias)
        bottoms.append(bottom if keep is None else jnp.where(keep, bottom, 0.0))
    copies = jnp.concatenate(bottoms * 2, axis=0).astype(jnp.bfloat16)
    size = copies.shape[0]
    for c in range(copies_ref.shape[0] // size):
        copies_ref[c * size : (c + 1) * size] = copies


def third_kernel(bottom_ref, stacked_ref, third_ref, copies_ref):
    share, cells = third_ref.shape
    depths = 3
    chans = bottom_ref.shape[0] // (depths * share)
    wide = stacked_ref.shape[2] // depths
    gathered = bottom_ref[...].astype(jnp.float32)
    blocks = []
    for k in range(depths):
        for c in turned(chans, chans - FIRST_CHAN):
            at = (c * depths + k) * share
            blocks.append(gathered[at : at + share])
        blocks.append(jnp.zeros((wide - chans * share, cells), jnp.float32))
    bottom = jnp.concatenate(blocks, axis=0).astype(jnp.bfloat16)
    taps = dot(stacked_ref[...].reshape(9 * PAIR, bottom.shape[0]), bottom)
    third = shift_add(taps, PAIR, HALF_ROWS, HALF_COLS)[:share]
    third_ref[...] = third
    copies_ref[...] = jnp.broadcast_to(own_statistics(third), copies_ref.shape)


def last_kernel(rows_ref, third_ref, gain_ref, bias_ref, out_ref):
    n = third_ref.shape[0]
    mean, spread = column_statistics(rows_ref[...], n)
    gain = to_column(gain_ref[...], 0, n)
    bias = to_column(bias_ref[...], 0, n)
    scale = gain * lax.rsqrt(spread + EPSILON)
    out_ref[...] = leaky(scale * (third_ref[...] - mean) + bias).astype(jnp.bfloat16)


def slab():
    return 2 * lax.axis_index("chip") + lax.axis_index("core")


def across(value):
    count = 2 * lax.axis_size("chip")
    pairs = [(i, (i + 2 * (i % 2) - 1) % count) for i in range(count)]
    return lax.ppermute(value, ("chip", "core"), pairs)


def beside(value):
    return lax.ppermute(value, "core", [(0, 1), (1, 0)])


def turned(count, first):
    return [(first + i) % count for i in range(count)]


def exchange(copies, axes, order):
    return lax.all_to_all(copies, axes, 0, 0, axis_index_groups=[order], tiled=True)


def struct(shape, dtype=jnp.float32):
    return jax.ShapeDtypeStruct(shape, dtype)


def local(
    features,
    first_weight,
    first_gain,
    first_bias,
    down_weight,
    down_gain,
    down_bias,
    third_weight,
    third_gain,
    third_bias,
):
    chips, chans = lax.axis_size("chip"), lax.axis_size("chan")
    in_chans = features.shape[0]
    n = first_weight.shape[1]
    m = third_weight.shape[1]
    wide = down_weight.shape[1]
    first_weight = first_weight.reshape(27 * n, in_chans)
    down_weight = jnp.transpose(down_weight, (0, 2, 1)).reshape(27 * n, wide)
    gains = [v.reshape(1, -1) for v in (first_gain, down_gain, third_gain)]
    biases = [v.reshape(1, -1) for v in (first_bias, down_bias, third_bias)]
    unit = 2 * 9 * n * in_chans * CELLS

    slices, weights, kept, cross, pair = kernel_call(
        send_kernel,
        (
            struct((2, in_chans, CELLS), jnp.bfloat16),
            struct(first_weight.shape, jnp.bfloat16),
            struct((2, n, CELLS)),
            struct((2, n, CELLS), jnp.bfloat16),
            struct((2, n, CELLS), jnp.bfloat16),
        ),
        (
            pltpu.with_memory_space_constraint(features, pltpu.HBM),
            pltpu.with_memory_space_constraint(first_weight, pltpu.HBM),
        ),
        4 * unit,
        "send",
        in_specs=[HBM, HBM],
        scratch=[
            pltpu.VMEM(features.shape, jnp.bfloat16),
            pltpu.SemaphoreType.DMA((2,)),
        ],
    )
    got_cross, got_pair = across(cross), beside(pair)
    own, select, stacked = kernel_call(
        own_kernel,
        (
            struct((n, CELLS)),
            struct((9 * HALF_CELLS, CELLS), jnp.bfloat16),
            struct((9, PAIR, 3 * 3 * LANES), jnp.bfloat16),
        ),
        (slices, weights, third_weight),
        2 * unit,
        "own",
    )
    first, copies = kernel_call(
        total_kernel,
        (struct((3, n, CELLS)), struct((2 * chips, LANES))),
        (kept, own, got_cross, got_pair),
        1 << 20,
        "total",
    )
    rows = exchange(copies, ("chip", "core"), turned(2 * chips, 2 * FIRST_CHIP))
    parts = kernel_call(
        down_kernel,
        struct((2 * chans * m, HALF_CELLS), jnp.bfloat16),
        (rows, first, gains[0], biases[0], select, down_weight),
        unit,
        "down",
    )
    parts = exchange(
        parts,
        ("core", "chan"),
        [core * chans + c for core in range(2) for c in turned(chans, FIRST_CHAN)],
    )
    reduced, mine, copies = kernel_call(
        reduced_kernel,
        (struct((2, m, HALF_CELLS)), struct((m, HALF_CELLS)), struct((chips, LANES))),
        (parts,),
        1 << 20,
        "reduced",
    )
    got = across(mine)
    rows = exchange(copies, "chip", turned(chips, SECOND_CHIP))
    copies = kernel_call(
        bottom_kernel,
        struct((chans * 3 * m, HALF_CELLS), jnp.bfloat16),
        (rows, reduced, got, gains[1], biases[1]),
        1 << 20,
        "bottom",
    )
    bottom = exchange(copies, "chan", turned(chans, FIRST_CHAN))
    third, copies = kernel_call(
        third_kernel,
        (struct((m, HALF_CELLS)), struct((2 * chips, LANES))),
        (bottom, stacked),
        unit,
        "third",
    )
    rows = exchange(copies, ("chip", "core"), turned(2 * chips, 2 * THIRD_CHIP))
    out = kernel_call(
        last_kernel,
        struct((m, HALF_CELLS), jnp.bfloat16),
        (rows, third, gains[2], biases[2]),
        1 << 20,
        "last",
    )
    return out.reshape(m, 1, HALF_CELLS)


def solution(mesh):
    chans = mesh.shape["chan"]
    pairs = jax.sharding.Mesh(mesh.devices.reshape(-1, 2, chans), ("chip", "core", "chan"))
    space = ("chip", "core")
    return jax.shard_map(
        local,
        mesh=pairs,
        in_specs=(
            P(None, space, None),
            P(None, "chan", None),
            P("chan"),
            P("chan"),
            P(None, None, "chan"),
            P("chan"),
            P("chan"),
            P(None, "chan", None),
            P("chan"),
            P("chan"),
        ),
        out_specs=P("chan", space, None),
        check_vma=False,
    )
```

```python
import jax
import jax.numpy as jnp
from jax import lax
from jax.experimental import pallas as pl
from jax.experimental.pallas import tpu as pltpu
from jax.sharding import PartitionSpec as P

ROWS = 16
COLS = 32
CELLS = ROWS * COLS
HALF_ROWS = ROWS // 2
HALF_COLS = COLS // 2
HALF_CELLS = HALF_ROWS * HALF_COLS
LANES = 128
PAIR = 48
FIRST_CHIP = 31
SECOND_CHIP = 0
THIRD_CHIP = 20
FIRST_CHAN = 4
EPSILON = 1e-05
SLOPE = 0.01

VMEM = pl.BlockSpec(memory_space=pltpu.VMEM)
HBM = pl.BlockSpec(memory_space=pltpu.HBM)


def kernel_call(body, outputs, operands, flops, name, in_specs=None, scratch=()):
    return pl.pallas_call(
        body,
        out_shape=outputs,
        in_specs=in_specs or [VMEM] * len(operands),
        out_specs=jax.tree.map(lambda _: VMEM, outputs),
        scratch_shapes=scratch,
        compiler_params=pltpu.CompilerParams(vmem_limit_bytes=32 * 1024 * 1024),
        cost_estimate=pl.CostEstimate(flops=flops, bytes_accessed=2 << 20, transcendentals=0),
        name=name,
    )(*operands)


def iota(shape, dim):
    return lax.broadcasted_iota(jnp.int32, shape, dim)


def dot(a, b):
    return jnp.dot(a, b, preferred_element_type=jnp.float32)


def dot_nt(a, b):
    return lax.dot_general(a, b, (((1,), (1,)), ((), ())), preferred_element_type=jnp.float32)


def to_row(column, offset):
    n = column.shape[0]
    hit = iota((n, LANES), 1) == iota((n, LANES), 0) + offset
    return jnp.sum(jnp.where(hit, column, 0.0), axis=0, keepdims=True)


def to_column(row, offset, n):
    width = row.shape[1]
    hit = iota((n, width), 1) == iota((n, width), 0) + offset
    return jnp.sum(jnp.where(hit, row, 0.0), axis=1, keepdims=True)


def shift_add(taps, out_chans, row_count, col_count):
    cells = row_count * col_count
    block = 3 * out_chans
    cell = iota((block, cells), 1)
    above = pltpu.roll(taps[:block], col_count, axis=1)
    below = pltpu.roll(taps[2 * block :], cells - col_count, axis=1)
    rows = (
        taps[block : 2 * block]
        + jnp.where(cell >= col_count, above, 0.0)
        + jnp.where(cell < cells - col_count, below, 0.0)
    )
    column = iota((out_chans, cells), 1) % col_count
    left = pltpu.roll(rows[:out_chans], 1, axis=1)
    right = pltpu.roll(rows[2 * out_chans :], cells - 1, axis=1)
    return (
        rows[out_chans : 2 * out_chans]
        + jnp.where(column != 0, left, 0.0)
        + jnp.where(column != col_count - 1, right, 0.0)
    )


def leaky(value):
    return jnp.where(value >= 0, value, SLOPE * value)


def send_kernel(
    features_hbm, weight_hbm,
    slices_ref, weight_ref, kept_ref, up_ref,
    features_ref, sems,
):
    loads = [
        pltpu.make_async_copy(features_hbm, features_ref, sems.at[0]),
        pltpu.make_async_copy(weight_hbm, weight_ref, sems.at[1]),
    ]
    for load in loads:
        load.start()
    chans = features_ref.shape[0]
    loads[0].wait()
    pairs = features_ref[...].reshape(2 * chans, CELLS)
    for j in range(2):
        pick = (iota((chans, 2 * chans), 1) == 2 * iota((chans, 2 * chans), 0) + j).astype(
            jnp.bfloat16
        )
        slices_ref[j] = dot(pick, pairs).astype(jnp.bfloat16)
    block = weight_ref.shape[0] // 3
    out_chans = block // 9
    lower, upper = slices_ref[0], slices_ref[1]
    loads[1].wait()
    tap0, tap1 = (weight_ref[k * block : (k + 1) * block] for k in range(2))
    up0 = shift_add(dot(tap0, lower) + dot(tap1, upper), out_chans, ROWS, COLS)
    kept_ref[...] = up0
    up_ref[0] = up0.astype(jnp.bfloat16)
    up_ref[1] = shift_add(dot(tap0, upper), out_chans, ROWS, COLS).astype(jnp.bfloat16)


def own_kernel(
    slices_ref, weight_ref, third_ref, own_ref, down_ref, below_ref, select_ref, stacked_ref
):
    block = weight_ref.shape[0] // 3
    out_chans = block // 9
    lower, upper = slices_ref[0], slices_ref[1]
    tap1, tap2 = weight_ref[block : 2 * block], weight_ref[2 * block :]
    down = shift_add(dot(tap2, lower), out_chans, ROWS, COLS)
    down = jnp.where(slab() == 0, 0.0, down)
    down_ref[...] = down
    below_ref[...] = down.astype(below_ref.dtype)
    own_ref[...] = shift_add(dot(tap1, lower) + dot(tap2, upper), out_chans, ROWS, COLS)

    place = iota((HALF_CELLS, CELLS), 0)
    cell = iota((HALF_CELLS, CELLS), 1)
    row, column = cell // COLS, cell % COLS
    row_gap = row - 2 * (place // HALF_COLS)
    column_gap = column - 2 * (place % HALF_COLS)
    for tap in range(9):
        hit = (row_gap == tap // 3 - 1) & (column_gap == tap % 3 - 1)
        select_ref[tap * HALF_CELLS : (tap + 1) * HALF_CELLS] = hit.astype(jnp.bfloat16)

    third_out, third_in = third_ref.shape[1:]
    stacked_ref[...] = jnp.zeros_like(stacked_ref)
    wide = stacked_ref.shape[2] // 3
    for depth in range(3):
        for tap in range(9):
            stacked_ref[tap, :third_out, depth * wide : depth * wide + third_in] = third_ref[
                depth * 9 + tap
            ]


def total_kernel(down_ref, own_ref, got_ref, first_ref, copies_ref):
    got = got_ref[...].astype(jnp.float32)
    first0 = down_ref[...] + got[0]
    first1 = own_ref[...] + jnp.where(slab() == 0, 0.0, got[1])
    first_ref[0] = first0
    first_ref[1] = first1
    cells = 2 * CELLS
    mean = (
        jnp.sum(first0, axis=1, keepdims=True) + jnp.sum(first1, axis=1, keepdims=True)
    ) / cells
    spread = (
        jnp.sum((first0 - mean) ** 2, axis=1, keepdims=True)
        + jnp.sum((first1 - mean) ** 2, axis=1, keepdims=True)
    ) / cells
    row = to_row(mean, 0) + to_row(spread, mean.shape[0])
    copies_ref[...] = jnp.broadcast_to(row, copies_ref.shape)


def column_statistics(rows, n):
    average = jnp.mean(rows, axis=0, keepdims=True)
    apart = jnp.mean((rows - average) ** 2, axis=0, keepdims=True)
    mean = to_column(average, 0, n)
    spread = to_column(average, n, n) + to_column(apart, 0, n)
    return mean, spread


def down_kernel(
    rows_ref, first_ref, kept_ref, back_ref, gain_ref, bias_ref, select_ref, weight_ref,
    parts_ref,
):
    n = first_ref.shape[1]
    mean, spread = column_statistics(rows_ref[...], n)
    gain = to_column(gain_ref[...], 0, n)
    bias = to_column(bias_ref[...], 0, n)
    scale = gain * lax.rsqrt(spread + EPSILON)
    firsts = (first_ref[0], first_ref[1], kept_ref[...] + back_ref[...].astype(jnp.float32))
    levels = [leaky(scale * (first - mean) + bias) for first in firsts]
    levels[0] = jnp.where(slab() == 0, 0.0, levels[0])
    levels.append(jnp.zeros((LANES - 3 * n, CELLS), jnp.float32))
    layers = jnp.concatenate(levels, axis=0).astype(jnp.bfloat16)
    out_chans = weight_ref.shape[1]
    picked = dot_nt(select_ref[...], layers).astype(jnp.bfloat16)
    windows, weights = [], []
    for tap in range(9):
        windows.append(picked[tap * HALF_CELLS : (tap + 1) * HALF_CELLS])
        for depth in range(3):
            at = (depth * 9 + tap) * n
            weights.append(weight_ref[at : at + n])
        weights.append(jnp.zeros((LANES - 3 * n, out_chans), jnp.bfloat16))
    parts = dot(jnp.concatenate(windows, axis=1), jnp.concatenate(weights, axis=0))
    spare = -out_chans % LANES
    parts = jnp.concatenate([parts, jnp.zeros((HALF_CELLS, spare), jnp.float32)], axis=1).T
    chans = lax.axis_size("chan")
    share = out_chans // chans
    parts = jnp.concatenate(
        [parts[c * share : (c + 1) * share] for c in turned(chans, FIRST_CHAN)], axis=0
    ).astype(jnp.bfloat16)
    for core in range(2):
        parts_ref[core * out_chans : (core + 1) * out_chans] = parts


def own_statistics(value):
    cells = value.shape[1]
    mean = jnp.sum(value, axis=1, keepdims=True) / cells
    spread = jnp.sum((value - mean) ** 2, axis=1, keepdims=True) / cells
    return to_row(mean, 0) + to_row(spread, value.shape[0])


def reduced_kernel(parts_ref, reduced_ref, mine_ref, copies_ref):
    share = reduced_ref.shape[1]
    parts = parts_ref[...].astype(jnp.float32)
    chans = parts.shape[0] // (2 * share)
    totals = []
    for core in range(2):
        shares = [
            parts[(core * chans + c) * share : (core * chans + c + 1) * share]
            for c in range(chans)
        ]
        totals.append(sum(shares[1:], shares[0]))
        reduced_ref[core] = totals[core]
    mine_ref[...] = jnp.where(lax.axis_index("core") == 0, totals[0], totals[1])
    row = own_statistics(jnp.concatenate(totals, axis=1))
    copies_ref[...] = jnp.broadcast_to(row, copies_ref.shape)


def bottom_kernel(rows_ref, reduced_ref, got_ref, gain_ref, bias_ref, copies_ref):
    n = got_ref.shape[0]
    mean, spread = column_statistics(rows_ref[...], n)
    gain = to_column(gain_ref[...], 0, n)
    bias = to_column(bias_ref[...], 0, n)
    scale = gain * lax.rsqrt(spread + EPSILON)
    even = lax.axis_index("core") == 0
    space = slab()
    last = 2 * lax.axis_size("chip") - 1
    got, reduced0, reduced1 = got_ref[...], reduced_ref[0], reduced_ref[1]
    slices = (
        (jnp.where(even, got, reduced0), space != 0),
        (jnp.where(even, reduced0, reduced1), None),
        (jnp.where(even, reduced1, got), space != last),
    )
    bottoms = []
    for value, keep in slices:
        bottom = leaky(scale * (value - mean) + bias)
        bottoms.append(bottom if keep is None else jnp.where(keep, bottom, 0.0))
    copies = jnp.concatenate(bottoms * 2, axis=0).astype(jnp.bfloat16)
    size = copies.shape[0]
    for c in range(copies_ref.shape[0] // size):
        copies_ref[c * size : (c + 1) * size] = copies


def third_kernel(bottom_ref, stacked_ref, third_ref, copies_ref):
    share, cells = third_ref.shape
    depths = 3
    chans = bottom_ref.shape[0] // (depths * share)
    wide = stacked_ref.shape[2] // depths
    gathered = bottom_ref[...].astype(jnp.float32)
    blocks = []
    for k in range(depths):
        for c in turned(chans, chans - FIRST_CHAN):
            at = (c * depths + k) * share
            blocks.append(gathered[at : at + share])
        blocks.append(jnp.zeros((wide - chans * share, cells), jnp.float32))
    bottom = jnp.concatenate(blocks, axis=0).astype(jnp.bfloat16)
    taps = dot(stacked_ref[...].reshape(9 * PAIR, bottom.shape[0]), bottom)
    third = shift_add(taps, PAIR, HALF_ROWS, HALF_COLS)[:share]
    third_ref[...] = third
    copies_ref[...] = jnp.broadcast_to(own_statistics(third), copies_ref.shape)


def last_kernel(rows_ref, third_ref, gain_ref, bias_ref, out_ref):
    n = third_ref.shape[0]
    mean, spread = column_statistics(rows_ref[...], n)
    gain = to_column(gain_ref[...], 0, n)
    bias = to_column(bias_ref[...], 0, n)
    scale = gain * lax.rsqrt(spread + EPSILON)
    out_ref[...] = leaky(scale * (third_ref[...] - mean) + bias).astype(jnp.bfloat16)


def slab():
    return 2 * lax.axis_index("chip") + lax.axis_index("core")


def across(value):
    count = 2 * lax.axis_size("chip")
    pairs = [(i, (i + 2 * (i % 2) - 1) % count) for i in range(count)]
    return lax.ppermute(value, ("chip", "core"), pairs)


def shift(value, by):
    count = 2 * lax.axis_size("chip")
    pairs = [(i, (i + by) % count) for i in range(count)]
    return lax.ppermute(value, ("chip", "core"), pairs)


def turned(count, first):
    return [(first + i) % count for i in range(count)]


def exchange(copies, axes, order):
    return lax.all_to_all(copies, axes, 0, 0, axis_index_groups=[order], tiled=True)


def struct(shape, dtype=jnp.float32):
    return jax.ShapeDtypeStruct(shape, dtype)


def local(
    features,
    first_weight,
    first_gain,
    first_bias,
    down_weight,
    down_gain,
    down_bias,
    third_weight,
    third_gain,
    third_bias,
):
    chips, chans = lax.axis_size("chip"), lax.axis_size("chan")
    in_chans = features.shape[0]
    n = first_weight.shape[1]
    m = third_weight.shape[1]
    wide = down_weight.shape[1]
    first_weight = first_weight.reshape(27 * n, in_chans)
    down_weight = jnp.transpose(down_weight, (0, 2, 1)).reshape(27 * n, wide)
    gains = [v.reshape(1, -1) for v in (first_gain, down_gain, third_gain)]
    biases = [v.reshape(1, -1) for v in (first_bias, down_bias, third_bias)]
    unit = 2 * 9 * n * in_chans * CELLS

    slices, weights, kept, up = kernel_call(
        send_kernel,
        (
            struct((2, in_chans, CELLS), jnp.bfloat16),
            struct(first_weight.shape, jnp.bfloat16),
            struct((n, CELLS)),
            struct((2, n, CELLS), jnp.bfloat16),
        ),
        (
            pltpu.with_memory_space_constraint(features, pltpu.HBM),
            pltpu.with_memory_space_constraint(first_weight, pltpu.HBM),
        ),
        4 * unit,
        "send",
        in_specs=[HBM, HBM],
        scratch=[
            pltpu.VMEM(features.shape, jnp.bfloat16),
            pltpu.SemaphoreType.DMA((2,)),
        ],
    )
    got = shift(up, 1)
    own, down, below, select, stacked = kernel_call(
        own_kernel,
        (
            struct((n, CELLS)),
            struct((n, CELLS)),
            struct((n, CELLS), jnp.float32),
            struct((9 * HALF_CELLS, CELLS), jnp.bfloat16),
            struct((9, PAIR, 3 * 3 * LANES), jnp.bfloat16),
        ),
        (slices, weights, third_weight),
        2 * unit,
        "own",
    )
    back = shift(below, -1)
    first, copies = kernel_call(
        total_kernel,
        (struct((2, n, CELLS)), struct((2 * chips, LANES))),
        (down, own, got),
        1 << 20,
        "total",
    )
    rows = lax.cond(
        slab() < 2 * chips,
        lambda sent: exchange(sent, ("chip", "core"), turned(2 * chips, 2 * FIRST_CHIP)),
        lambda sent: sent,
        copies,
    )
    parts = kernel_call(
        down_kernel,
        struct((2 * chans * m, HALF_CELLS), jnp.bfloat16),
        (rows, first, kept, back, gains[0], biases[0], select, down_weight),
        unit,
        "down",
    )
    parts = exchange(
        parts,
        ("core", "chan"),
        [core * chans + c for core in range(2) for c in turned(chans, FIRST_CHAN)],
    )
    reduced, mine, copies = kernel_call(
        reduced_kernel,
        (struct((2, m, HALF_CELLS)), struct((m, HALF_CELLS)), struct((chips, LANES))),
        (parts,),
        1 << 20,
        "reduced",
    )
    got = across(mine)
    rows = exchange(copies, "chip", turned(chips, SECOND_CHIP))
    copies = kernel_call(
        bottom_kernel,
        struct((chans * 3 * m, HALF_CELLS), jnp.bfloat16),
        (rows, reduced, got, gains[1], biases[1]),
        1 << 20,
        "bottom",
    )
    bottom = exchange(copies, "chan", turned(chans, FIRST_CHAN))
    third, copies = kernel_call(
        third_kernel,
        (struct((m, HALF_CELLS)), struct((2 * chips, LANES))),
        (bottom, stacked),
        unit,
        "third",
    )
    rows = exchange(copies, ("chip", "core"), turned(2 * chips, 2 * THIRD_CHIP))
    out = kernel_call(
        last_kernel,
        struct((m, HALF_CELLS), jnp.bfloat16),
        (rows, third, gains[2], biases[2]),
        1 << 20,
        "last",
    )
    return out.reshape(m, 1, HALF_CELLS)


def solution(mesh):
    chans = mesh.shape["chan"]
    pairs = jax.sharding.Mesh(mesh.devices.reshape(-1, 2, chans), ("chip", "core", "chan"))
    space = ("chip", "core")
    return jax.shard_map(
        local,
        mesh=pairs,
        in_specs=(
            P(None, space, None),
            P(None, "chan", None),
            P("chan"),
            P("chan"),
            P(None, None, "chan"),
            P("chan"),
            P("chan"),
            P(None, "chan", None),
            P("chan"),
            P("chan"),
        ),
        out_specs=P("chan", space, None),
        check_vma=False,
    )
```

```python
import jax
import jax.numpy as jnp
from jax import lax
from jax.experimental import pallas as pl
from jax.experimental.pallas import tpu as pltpu
from jax.sharding import PartitionSpec as P

ROWS = 16
COLS = 32
CELLS = ROWS * COLS
HALF_ROWS = ROWS // 2
HALF_COLS = COLS // 2
HALF_CELLS = HALF_ROWS * HALF_COLS
LANES = 128
PAIR = 48
FIRST_CHIP = 31
SECOND_CHIP = 7
THIRD_CHIP = 20
FIRST_CHAN = 5
SECOND_CHAN = 5
EPSILON = 1e-05
SLOPE = 0.01

VMEM = pl.BlockSpec(memory_space=pltpu.VMEM)
HBM = pl.BlockSpec(memory_space=pltpu.HBM)


def kernel_call(body, outputs, operands, flops, name, in_specs=None, scratch=()):
    return pl.pallas_call(
        body,
        out_shape=outputs,
        in_specs=in_specs or [VMEM] * len(operands),
        out_specs=jax.tree.map(lambda _: VMEM, outputs),
        scratch_shapes=scratch,
        compiler_params=pltpu.CompilerParams(vmem_limit_bytes=32 * 1024 * 1024),
        cost_estimate=pl.CostEstimate(flops=flops, bytes_accessed=2 << 20, transcendentals=0),
        name=name,
    )(*operands)


def iota(shape, dim):
    return lax.broadcasted_iota(jnp.int32, shape, dim)


def dot(a, b):
    return jnp.dot(a, b, preferred_element_type=jnp.float32)


def dot_nt(a, b):
    return lax.dot_general(a, b, (((1,), (1,)), ((), ())), preferred_element_type=jnp.float32)


def to_row(column, offset):
    n = column.shape[0]
    hit = iota((n, LANES), 1) == iota((n, LANES), 0) + offset
    return jnp.sum(jnp.where(hit, column, 0.0), axis=0, keepdims=True)


def to_column(row, offset, n):
    width = row.shape[1]
    hit = iota((n, width), 1) == iota((n, width), 0) + offset
    return jnp.sum(jnp.where(hit, row, 0.0), axis=1, keepdims=True)


def shift_add(taps, out_chans, row_count, col_count):
    cells = row_count * col_count
    block = 3 * out_chans
    cell = iota((block, cells), 1)
    above = pltpu.roll(taps[:block], col_count, axis=1)
    below = pltpu.roll(taps[2 * block :], cells - col_count, axis=1)
    rows = (
        taps[block : 2 * block]
        + jnp.where(cell >= col_count, above, 0.0)
        + jnp.where(cell < cells - col_count, below, 0.0)
    )
    column = iota((out_chans, cells), 1) % col_count
    left = pltpu.roll(rows[:out_chans], 1, axis=1)
    right = pltpu.roll(rows[2 * out_chans :], cells - 1, axis=1)
    return (
        rows[out_chans : 2 * out_chans]
        + jnp.where(column != 0, left, 0.0)
        + jnp.where(column != col_count - 1, right, 0.0)
    )


def leaky(value):
    return jnp.where(value >= 0, value, SLOPE * value)


def send_kernel(
    features_hbm, weight_hbm,
    slices_ref, weight_ref, kept_ref, up_ref,
    features_ref, sems,
):
    loads = [
        pltpu.make_async_copy(features_hbm, features_ref, sems.at[0]),
        pltpu.make_async_copy(weight_hbm, weight_ref, sems.at[1]),
    ]
    for load in loads:
        load.start()
    chans = features_ref.shape[0]
    gap = iota((chans, 2 * chans), 1) - 2 * iota((chans, 2 * chans), 0)
    picks = [(gap == j).astype(jnp.bfloat16) for j in range(2)]
    loads[0].wait()
    pairs = features_ref[...].reshape(2 * chans, CELLS)
    for j in range(2):
        slices_ref[j] = dot(picks[j], pairs).astype(jnp.bfloat16)
    block = weight_ref.shape[0] // 3
    out_chans = block // 9
    lower, upper = slices_ref[0], slices_ref[1]
    loads[1].wait()
    tap0, tap1 = (weight_ref[k * block : (k + 1) * block] for k in range(2))
    up0 = shift_add(dot(tap0, lower) + dot(tap1, upper), out_chans, ROWS, COLS)
    kept_ref[...] = up0
    up_ref[0] = up0.astype(jnp.bfloat16)
    up_ref[1] = shift_add(dot(tap0, upper), out_chans, ROWS, COLS).astype(jnp.bfloat16)


def own_kernel(
    slices_ref, weight_ref, third_ref, own_ref, down_ref, below_ref, select_ref, stacked_ref
):
    block = weight_ref.shape[0] // 3
    out_chans = block // 9
    lower, upper = slices_ref[0], slices_ref[1]
    tap1, tap2 = weight_ref[block : 2 * block], weight_ref[2 * block :]
    down = shift_add(dot(tap2, lower), out_chans, ROWS, COLS)
    down = jnp.where(slab() == 0, 0.0, down)
    down_ref[...] = down
    below_ref[...] = down.astype(below_ref.dtype)
    own_ref[...] = shift_add(dot(tap1, lower) + dot(tap2, upper), out_chans, ROWS, COLS)

    cell = iota((CELLS, HALF_CELLS), 0)
    place = iota((CELLS, HALF_CELLS), 1)
    row_gap = cell // COLS - 2 * (place // HALF_COLS)
    column_gap = cell % COLS - 2 * (place % HALF_COLS)
    gap = row_gap * (2 * COLS) + column_gap
    for tap in range(9):
        hit = gap == (tap // 3 - 1) * (2 * COLS) + tap % 3 - 1
        select_ref[:, tap * HALF_CELLS : (tap + 1) * HALF_CELLS] = hit.astype(jnp.bfloat16)

    third_out, third_in = third_ref.shape[1:]
    stacked_ref[...] = jnp.zeros_like(stacked_ref)
    wide = stacked_ref.shape[2] // 3
    for depth in range(3):
        for tap in range(9):
            stacked_ref[tap, :third_out, depth * wide : depth * wide + third_in] = third_ref[
                depth * 9 + tap
            ]


def total_kernel(down_ref, own_ref, got_ref, first_ref, copies_ref):
    got = got_ref[...].astype(jnp.float32)
    first0 = down_ref[...] + got[0]
    first1 = own_ref[...] + jnp.where(slab() == 0, 0.0, got[1])
    first_ref[0] = first0
    first_ref[1] = first1
    cells = 2 * CELLS
    mean = (
        jnp.sum(first0, axis=1, keepdims=True) + jnp.sum(first1, axis=1, keepdims=True)
    ) / cells
    spread = (
        jnp.sum((first0 - mean) ** 2, axis=1, keepdims=True)
        + jnp.sum((first1 - mean) ** 2, axis=1, keepdims=True)
    ) / cells
    row = to_row(mean, 0) + to_row(spread, mean.shape[0])
    copies_ref[...] = jnp.broadcast_to(row, copies_ref.shape)


def column_statistics(rows, n):
    average = jnp.mean(rows, axis=0, keepdims=True)
    apart = jnp.mean((rows - average) ** 2, axis=0, keepdims=True)
    mean = to_column(average, 0, n)
    spread = to_column(average, n, n) + to_column(apart, 0, n)
    return mean, spread


def down_kernel(
    rows_ref, first_ref, kept_ref, back_ref, gain_ref, bias_ref, select_ref, weight_ref,
    parts_ref,
):
    n = first_ref.shape[1]
    mean, spread = column_statistics(rows_ref[...], n)
    gain = to_column(gain_ref[...], 0, n)
    bias = to_column(bias_ref[...], 0, n)
    scale = gain * lax.rsqrt(spread + EPSILON)
    firsts = (first_ref[0], first_ref[1], kept_ref[...] + back_ref[...].astype(jnp.float32))
    levels = [leaky(scale * (first - mean) + bias) for first in firsts]
    levels[0] = jnp.where(slab() == 0, 0.0, levels[0])
    layers = jnp.concatenate(levels, axis=0).astype(jnp.bfloat16)
    out_chans = weight_ref.shape[1]
    picked = dot(layers, select_ref[...]).astype(jnp.bfloat16)
    windows = jnp.concatenate(
        [
            picked[depth * n : (depth + 1) * n, tap * HALF_CELLS : (tap + 1) * HALF_CELLS]
            for depth in range(3)
            for tap in range(9)
        ],
        axis=0,
    )
    parts = lax.dot_general(
        windows, weight_ref[...], (((0,), (0,)), ((), ())), preferred_element_type=jnp.float32
    )
    spare = -out_chans % LANES
    parts = jnp.concatenate([parts, jnp.zeros((HALF_CELLS, spare), jnp.float32)], axis=1).T
    chans = lax.axis_size("chan")
    share = out_chans // chans
    parts = jnp.concatenate(
        [parts[c * share : (c + 1) * share] for c in turned(chans, FIRST_CHAN)], axis=0
    ).astype(jnp.bfloat16)
    for core in range(2):
        parts_ref[core * out_chans : (core + 1) * out_chans] = parts


def own_statistics(value):
    cells = value.shape[1]
    mean = jnp.sum(value, axis=1, keepdims=True) / cells
    spread = jnp.sum((value - mean) ** 2, axis=1, keepdims=True) / cells
    return to_row(mean, 0) + to_row(spread, value.shape[0])


def reduced_kernel(parts_ref, reduced_ref, mine_ref, copies_ref):
    share = reduced_ref.shape[1]
    parts = parts_ref[...].astype(jnp.float32)
    chans = parts.shape[0] // (2 * share)
    totals = []
    for core in range(2):
        shares = [
            parts[(core * chans + c) * share : (core * chans + c + 1) * share]
            for c in range(chans)
        ]
        totals.append(sum(shares[1:], shares[0]))
        reduced_ref[core] = totals[core]
    mine_ref[...] = jnp.where(lax.axis_index("core") == 0, totals[0], totals[1])
    row = own_statistics(jnp.concatenate(totals, axis=1))
    copies_ref[...] = jnp.broadcast_to(row, copies_ref.shape)


def bottom_kernel(rows_ref, reduced_ref, got_ref, gain_ref, bias_ref, copies_ref):
    n = got_ref.shape[0]
    mean, spread = column_statistics(rows_ref[...], n)
    gain = to_column(gain_ref[...], 0, n)
    bias = to_column(bias_ref[...], 0, n)
    scale = gain * lax.rsqrt(spread + EPSILON)
    even = lax.axis_index("core") == 0
    space = slab()
    last = 2 * lax.axis_size("chip") - 1
    got, reduced0, reduced1 = got_ref[...], reduced_ref[0], reduced_ref[1]
    slices = (
        (jnp.where(even, got, reduced0), space != 0),
        (jnp.where(even, reduced0, reduced1), None),
        (jnp.where(even, reduced1, got), space != last),
    )
    bottoms = []
    for value, keep in slices:
        bottom = leaky(scale * (value - mean) + bias)
        bottoms.append(bottom if keep is None else jnp.where(keep, bottom, 0.0))
    copies = jnp.concatenate(bottoms * 2, axis=0).astype(jnp.bfloat16)
    size = copies.shape[0]
    for c in range(copies_ref.shape[0] // size):
        copies_ref[c * size : (c + 1) * size] = copies


def third_kernel(bottom_ref, stacked_ref, third_ref, copies_ref):
    share, cells = third_ref.shape
    depths = 3
    chans = bottom_ref.shape[0] // (depths * share)
    wide = stacked_ref.shape[2] // depths
    gathered = bottom_ref[...].astype(jnp.float32)
    blocks = []
    for k in range(depths):
        for c in turned(chans, chans - SECOND_CHAN):
            at = (c * depths + k) * share
            blocks.append(gathered[at : at + share])
        blocks.append(jnp.zeros((wide - chans * share, cells), jnp.float32))
    bottom = jnp.concatenate(blocks, axis=0).astype(jnp.bfloat16)
    taps = dot(stacked_ref[...].reshape(9 * PAIR, bottom.shape[0]), bottom)
    third = shift_add(taps, PAIR, HALF_ROWS, HALF_COLS)[:share]
    third_ref[...] = third
    copies_ref[...] = jnp.broadcast_to(own_statistics(third), copies_ref.shape)


def last_kernel(rows_ref, third_ref, gain_ref, bias_ref, out_ref):
    n = third_ref.shape[0]
    mean, spread = column_statistics(rows_ref[...], n)
    gain = to_column(gain_ref[...], 0, n)
    bias = to_column(bias_ref[...], 0, n)
    scale = gain * lax.rsqrt(spread + EPSILON)
    out_ref[...] = leaky(scale * (third_ref[...] - mean) + bias).astype(jnp.bfloat16)


def slab():
    return 2 * lax.axis_index("chip") + lax.axis_index("core")


def across(value):
    count = 2 * lax.axis_size("chip")
    pairs = [(i, (i + 2 * (i % 2) - 1) % count) for i in range(count)]
    return lax.ppermute(value, ("chip", "core"), pairs)


def shift(value, by):
    count = 2 * lax.axis_size("chip")
    pairs = [(i, (i + by) % count) for i in range(count)]
    return lax.ppermute(value, ("chip", "core"), pairs)


def turned(count, first):
    return [(first + i) % count for i in range(count)]


def exchange(copies, axes, order):
    return lax.all_to_all(copies, axes, 0, 0, axis_index_groups=[order], tiled=True)


def struct(shape, dtype=jnp.float32):
    return jax.ShapeDtypeStruct(shape, dtype)


def local(
    features,
    first_weight,
    first_gain,
    first_bias,
    down_weight,
    down_gain,
    down_bias,
    third_weight,
    third_gain,
    third_bias,
):
    chips, chans = lax.axis_size("chip"), lax.axis_size("chan")
    in_chans = features.shape[0]
    n = first_weight.shape[1]
    m = third_weight.shape[1]
    wide = down_weight.shape[1]
    first_weight = first_weight.reshape(27 * n, in_chans)
    down_weight = jnp.transpose(down_weight, (0, 2, 1)).reshape(27 * n, wide)
    gains = [v.reshape(1, -1) for v in (first_gain, down_gain, third_gain)]
    biases = [v.reshape(1, -1) for v in (first_bias, down_bias, third_bias)]
    unit = 2 * 9 * n * in_chans * CELLS

    slices, weights, kept, up = kernel_call(
        send_kernel,
        (
            struct((2, in_chans, CELLS), jnp.bfloat16),
            struct(first_weight.shape, jnp.bfloat16),
            struct((n, CELLS)),
            struct((2, n, CELLS), jnp.bfloat16),
        ),
        (
            pltpu.with_memory_space_constraint(features, pltpu.HBM),
            pltpu.with_memory_space_constraint(first_weight, pltpu.HBM),
        ),
        4 * unit,
        "send",
        in_specs=[HBM, HBM],
        scratch=[
            pltpu.VMEM(features.shape, jnp.bfloat16),
            pltpu.SemaphoreType.DMA((2,)),
        ],
    )
    got = shift(up, 1)
    own, down, below, select, stacked = kernel_call(
        own_kernel,
        (
            struct((n, CELLS)),
            struct((n, CELLS)),
            struct((n, CELLS), jnp.float32),
            struct((CELLS, 9 * HALF_CELLS), jnp.bfloat16),
            struct((9, PAIR, 3 * 3 * LANES), jnp.bfloat16),
        ),
        (slices, weights, third_weight),
        2 * unit,
        "own",
    )
    back = shift(below, -1)
    first, copies = kernel_call(
        total_kernel,
        (struct((2, n, CELLS)), struct((2 * chips, LANES))),
        (down, own, got),
        1 << 20,
        "total",
    )
    rows = lax.cond(
        slab() < 2 * chips,
        lambda sent: exchange(sent, ("chip", "core"), turned(2 * chips, 2 * FIRST_CHIP)),
        lambda sent: sent,
        copies,
    )
    parts = kernel_call(
        down_kernel,
        struct((2 * chans * m, HALF_CELLS), jnp.bfloat16),
        (rows, first, kept, back, gains[0], biases[0], select, down_weight),
        unit,
        "down",
    )
    parts = exchange(
        parts,
        ("core", "chan"),
        [core * chans + c for core in range(2) for c in turned(chans, FIRST_CHAN)],
    )
    reduced, mine, copies = kernel_call(
        reduced_kernel,
        (struct((2, m, HALF_CELLS)), struct((m, HALF_CELLS)), struct((chips, LANES))),
        (parts,),
        1 << 20,
        "reduced",
    )
    got = across(mine)
    rows = exchange(copies, "chip", turned(chips, SECOND_CHIP))
    copies = kernel_call(
        bottom_kernel,
        struct((chans * 3 * m, HALF_CELLS), jnp.bfloat16),
        (rows, reduced, got, gains[1], biases[1]),
        1 << 20,
        "bottom",
    )
    bottom = exchange(copies, "chan", turned(chans, SECOND_CHAN))
    third, copies = kernel_call(
        third_kernel,
        (struct((m, HALF_CELLS)), struct((2 * chips, LANES))),
        (bottom, stacked),
        unit,
        "third",
    )
    rows = exchange(copies, ("chip", "core"), turned(2 * chips, 2 * THIRD_CHIP))
    out = kernel_call(
        last_kernel,
        struct((m, HALF_CELLS), jnp.bfloat16),
        (rows, third, gains[2], biases[2]),
        1 << 20,
        "last",
    )
    return out.reshape(m, 1, HALF_CELLS)


def solution(mesh):
    chans = mesh.shape["chan"]
    pairs = jax.sharding.Mesh(mesh.devices.reshape(-1, 2, chans), ("chip", "core", "chan"))
    space = ("chip", "core")
    return jax.shard_map(
        local,
        mesh=pairs,
        in_specs=(
            P(None, space, None),
            P(None, "chan", None),
            P("chan"),
            P("chan"),
            P(None, None, "chan"),
            P("chan"),
            P("chan"),
            P(None, "chan", None),
            P("chan"),
            P("chan"),
        ),
        out_specs=P("chan", space, None),
        check_vma=False,
    )
```

```python
import jax
import jax.numpy as jnp
import ml_dtypes
import numpy as np
from jax import lax
from jax.experimental import pallas as pl
from jax.experimental.pallas import tpu as pltpu
from jax.sharding import PartitionSpec as P

ROWS = 16
COLS = 32
CELLS = ROWS * COLS
HALF_ROWS = ROWS // 2
HALF_COLS = COLS // 2
HALF_CELLS = HALF_ROWS * HALF_COLS
LANES = 128
PAIR = 48
FIRST_CHIP = 31
SECOND_CHIP = 7
THIRD_CHIP = 20
FIRST_CHAN = 5
SECOND_CHAN = 5
EPSILON = 1e-05
SLOPE = 0.01

VMEM = pl.BlockSpec(memory_space=pltpu.VMEM)
HBM = pl.BlockSpec(memory_space=pltpu.HBM)


def kernel_call(body, outputs, operands, flops, name, in_specs=None, scratch=()):
    return pl.pallas_call(
        body,
        out_shape=outputs,
        in_specs=in_specs or [VMEM] * len(operands),
        out_specs=jax.tree.map(lambda _: VMEM, outputs),
        scratch_shapes=scratch,
        compiler_params=pltpu.CompilerParams(vmem_limit_bytes=32 * 1024 * 1024),
        cost_estimate=pl.CostEstimate(flops=flops, bytes_accessed=2 << 20, transcendentals=0),
        name=name,
    )(*operands)


def iota(shape, dim):
    return lax.broadcasted_iota(jnp.int32, shape, dim)


def dot(a, b):
    return jnp.dot(a, b, preferred_element_type=jnp.float32)


def dot_nt(a, b):
    return lax.dot_general(a, b, (((1,), (1,)), ((), ())), preferred_element_type=jnp.float32)


def to_row(column, offset):
    n = column.shape[0]
    hit = iota((n, LANES), 1) == iota((n, LANES), 0) + offset
    return jnp.sum(jnp.where(hit, column, 0.0), axis=0, keepdims=True)


def to_column(row, offset, n):
    width = row.shape[1]
    hit = iota((n, width), 1) == iota((n, width), 0) + offset
    return jnp.sum(jnp.where(hit, row, 0.0), axis=1, keepdims=True)


def shift_add(taps, out_chans, row_count, col_count):
    cells = row_count * col_count
    block = 3 * out_chans
    cell = iota((block, cells), 1)
    above = pltpu.roll(taps[:block], col_count, axis=1)
    below = pltpu.roll(taps[2 * block :], cells - col_count, axis=1)
    rows = (
        taps[block : 2 * block]
        + jnp.where(cell >= col_count, above, 0.0)
        + jnp.where(cell < cells - col_count, below, 0.0)
    )
    column = iota((out_chans, cells), 1) % col_count
    left = pltpu.roll(rows[:out_chans], 1, axis=1)
    right = pltpu.roll(rows[2 * out_chans :], cells - 1, axis=1)
    return (
        rows[out_chans : 2 * out_chans]
        + jnp.where(column != 0, left, 0.0)
        + jnp.where(column != col_count - 1, right, 0.0)
    )


def leaky(value):
    return jnp.where(value >= 0, value, SLOPE * value)


def send_kernel(
    features_hbm, weight_hbm,
    slices_ref, weight_ref, kept_ref, up_ref,
    features_ref, sems,
):
    loads = [
        pltpu.make_async_copy(features_hbm, features_ref, sems.at[0]),
        pltpu.make_async_copy(weight_hbm, weight_ref, sems.at[1]),
    ]
    for load in loads:
        load.start()
    chans = features_ref.shape[0]
    gap = iota((chans, 2 * chans), 1) - 2 * iota((chans, 2 * chans), 0)
    picks = [(gap == j).astype(jnp.bfloat16) for j in range(2)]
    loads[0].wait()
    pairs = features_ref[...].reshape(2 * chans, CELLS)
    for j in range(2):
        slices_ref[j] = dot(picks[j], pairs).astype(jnp.bfloat16)
    block = weight_ref.shape[0] // 3
    out_chans = block // 9
    lower, upper = slices_ref[0], slices_ref[1]
    loads[1].wait()
    tap0, tap1 = (weight_ref[k * block : (k + 1) * block] for k in range(2))
    up0 = shift_add(dot(tap0, lower) + dot(tap1, upper), out_chans, ROWS, COLS)
    kept_ref[...] = up0
    up_ref[0] = up0.astype(jnp.bfloat16)
    up_ref[1] = shift_add(dot(tap0, upper), out_chans, ROWS, COLS).astype(jnp.bfloat16)


def own_kernel(
    slices_ref, weight_ref, third_ref, own_ref, down_ref, below_ref, stacked_ref
):
    block = weight_ref.shape[0] // 3
    out_chans = block // 9
    lower, upper = slices_ref[0], slices_ref[1]
    tap1, tap2 = weight_ref[block : 2 * block], weight_ref[2 * block :]
    down = shift_add(dot(tap2, lower), out_chans, ROWS, COLS)
    down = jnp.where(slab() == 0, 0.0, down)
    down_ref[...] = down
    below_ref[...] = down.astype(below_ref.dtype)
    own_ref[...] = shift_add(dot(tap1, lower) + dot(tap2, upper), out_chans, ROWS, COLS)

    third_out, third_in = third_ref.shape[1:]
    stacked_ref[...] = jnp.zeros_like(stacked_ref)
    wide = stacked_ref.shape[2] // 3
    for depth in range(3):
        for tap in range(9):
            stacked_ref[tap, :third_out, depth * wide : depth * wide + third_in] = third_ref[
                depth * 9 + tap
            ]


def total_kernel(down_ref, own_ref, got_ref, first_ref, copies_ref):
    got = got_ref[...].astype(jnp.float32)
    first0 = down_ref[...] + got[0]
    first1 = own_ref[...] + jnp.where(slab() == 0, 0.0, got[1])
    first_ref[0] = first0
    first_ref[1] = first1
    cells = 2 * CELLS
    mean = (
        jnp.sum(first0, axis=1, keepdims=True) + jnp.sum(first1, axis=1, keepdims=True)
    ) / cells
    spread = (
        jnp.sum((first0 - mean) ** 2, axis=1, keepdims=True)
        + jnp.sum((first1 - mean) ** 2, axis=1, keepdims=True)
    ) / cells
    row = to_row(mean, 0) + to_row(spread, mean.shape[0])
    copies_ref[...] = jnp.broadcast_to(row, copies_ref.shape)


def column_statistics(rows, n):
    average = jnp.mean(rows, axis=0, keepdims=True)
    apart = jnp.mean((rows - average) ** 2, axis=0, keepdims=True)
    mean = to_column(average, 0, n)
    spread = to_column(average, n, n) + to_column(apart, 0, n)
    return mean, spread


def down_kernel(
    rows_ref, first_ref, kept_ref, back_ref, gain_ref, bias_ref, select_ref, weight_ref,
    parts_ref,
):
    n = first_ref.shape[1]
    mean, spread = column_statistics(rows_ref[...], n)
    gain = to_column(gain_ref[...], 0, n)
    bias = to_column(bias_ref[...], 0, n)
    scale = gain * lax.rsqrt(spread + EPSILON)
    firsts = (first_ref[0], first_ref[1], kept_ref[...] + back_ref[...].astype(jnp.float32))
    levels = [leaky(scale * (first - mean) + bias) for first in firsts]
    levels[0] = jnp.where(slab() == 0, 0.0, levels[0])
    layers = jnp.concatenate(levels, axis=0).astype(jnp.bfloat16)
    out_chans = weight_ref.shape[1]
    picked = dot(layers, select_ref[...]).astype(jnp.bfloat16)
    windows = jnp.concatenate(
        [
            picked[depth * n : (depth + 1) * n, tap * HALF_CELLS : (tap + 1) * HALF_CELLS]
            for depth in range(3)
            for tap in range(9)
        ],
        axis=0,
    )
    parts = lax.dot_general(
        windows, weight_ref[...], (((0,), (0,)), ((), ())), preferred_element_type=jnp.float32
    )
    spare = -out_chans % LANES
    parts = jnp.concatenate([parts, jnp.zeros((HALF_CELLS, spare), jnp.float32)], axis=1).T
    chans = lax.axis_size("chan")
    share = out_chans // chans
    parts = jnp.concatenate(
        [parts[c * share : (c + 1) * share] for c in turned(chans, FIRST_CHAN)], axis=0
    ).astype(jnp.bfloat16)
    for core in range(2):
        parts_ref[core * out_chans : (core + 1) * out_chans] = parts


def own_statistics(value):
    cells = value.shape[1]
    mean = jnp.sum(value, axis=1, keepdims=True) / cells
    spread = jnp.sum((value - mean) ** 2, axis=1, keepdims=True) / cells
    return to_row(mean, 0) + to_row(spread, value.shape[0])


def reduced_kernel(parts_ref, reduced_ref, mine_ref, copies_ref):
    share = reduced_ref.shape[1]
    parts = parts_ref[...].astype(jnp.float32)
    chans = parts.shape[0] // (2 * share)
    totals = []
    for core in range(2):
        shares = [
            parts[(core * chans + c) * share : (core * chans + c + 1) * share]
            for c in range(chans)
        ]
        totals.append(sum(shares[1:], shares[0]))
        reduced_ref[core] = totals[core]
    mine_ref[...] = jnp.where(lax.axis_index("core") == 0, totals[0], totals[1])
    row = own_statistics(jnp.concatenate(totals, axis=1))
    copies_ref[...] = jnp.broadcast_to(row, copies_ref.shape)


def bottom_kernel(rows_ref, reduced_ref, got_ref, gain_ref, bias_ref, copies_ref):
    n = got_ref.shape[0]
    mean, spread = column_statistics(rows_ref[...], n)
    gain = to_column(gain_ref[...], 0, n)
    bias = to_column(bias_ref[...], 0, n)
    scale = gain * lax.rsqrt(spread + EPSILON)
    even = lax.axis_index("core") == 0
    space = slab()
    last = 2 * lax.axis_size("chip") - 1
    got, reduced0, reduced1 = got_ref[...], reduced_ref[0], reduced_ref[1]
    slices = (
        (jnp.where(even, got, reduced0), space != 0),
        (jnp.where(even, reduced0, reduced1), None),
        (jnp.where(even, reduced1, got), space != last),
    )
    bottoms = []
    for value, keep in slices:
        bottom = leaky(scale * (value - mean) + bias)
        bottoms.append(bottom if keep is None else jnp.where(keep, bottom, 0.0))
    copies = jnp.concatenate(bottoms * 2, axis=0).astype(jnp.bfloat16)
    size = copies.shape[0]
    for c in range(copies_ref.shape[0] // size):
        copies_ref[c * size : (c + 1) * size] = copies


def third_kernel(bottom_ref, stacked_ref, third_ref, copies_ref):
    share, cells = third_ref.shape
    depths = 3
    chans = bottom_ref.shape[0] // (depths * share)
    wide = stacked_ref.shape[2] // depths
    gathered = bottom_ref[...].astype(jnp.float32)
    blocks = []
    for k in range(depths):
        for c in turned(chans, chans - SECOND_CHAN):
            at = (c * depths + k) * share
            blocks.append(gathered[at : at + share])
        blocks.append(jnp.zeros((wide - chans * share, cells), jnp.float32))
    bottom = jnp.concatenate(blocks, axis=0).astype(jnp.bfloat16)
    taps = dot(stacked_ref[...].reshape(9 * PAIR, bottom.shape[0]), bottom)
    third = shift_add(taps, PAIR, HALF_ROWS, HALF_COLS)[:share]
    third_ref[...] = third
    copies_ref[...] = jnp.broadcast_to(own_statistics(third), copies_ref.shape)


def last_kernel(rows_ref, third_ref, gain_ref, bias_ref, out_ref):
    n = third_ref.shape[0]
    mean, spread = column_statistics(rows_ref[...], n)
    gain = to_column(gain_ref[...], 0, n)
    bias = to_column(bias_ref[...], 0, n)
    scale = gain * lax.rsqrt(spread + EPSILON)
    out_ref[...] = leaky(scale * (third_ref[...] - mean) + bias).astype(jnp.bfloat16)


def slab():
    return 2 * lax.axis_index("chip") + lax.axis_index("core")


def across(value):
    count = 2 * lax.axis_size("chip")
    pairs = [(i, (i + 2 * (i % 2) - 1) % count) for i in range(count)]
    return lax.ppermute(value, ("chip", "core"), pairs)


def shift(value, by):
    count = 2 * lax.axis_size("chip")
    pairs = [(i, (i + by) % count) for i in range(count)]
    return lax.ppermute(value, ("chip", "core"), pairs)


def turned(count, first):
    return [(first + i) % count for i in range(count)]


def exchange(copies, axes, order):
    return lax.all_to_all(copies, axes, 0, 0, axis_index_groups=[order], tiled=True)


def sampling():
    cell = np.arange(CELLS)[:, None, None]
    tap = np.arange(9)[None, :, None]
    place = np.arange(HALF_CELLS)[None, None, :]
    row = 2 * (place // HALF_COLS) + tap // 3 - 1
    column = 2 * (place % HALF_COLS) + tap % 3 - 1
    hit = (cell // COLS == row) & (cell % COLS == column)
    return hit.reshape(CELLS, 9 * HALF_CELLS).astype(ml_dtypes.bfloat16)


def struct(shape, dtype=jnp.float32):
    return jax.ShapeDtypeStruct(shape, dtype)


def local(
    features,
    first_weight,
    first_gain,
    first_bias,
    down_weight,
    down_gain,
    down_bias,
    third_weight,
    third_gain,
    third_bias,
):
    chips, chans = lax.axis_size("chip"), lax.axis_size("chan")
    in_chans = features.shape[0]
    n = first_weight.shape[1]
    m = third_weight.shape[1]
    wide = down_weight.shape[1]
    first_weight = first_weight.reshape(27 * n, in_chans)
    down_weight = jnp.transpose(down_weight, (0, 2, 1)).reshape(27 * n, wide)
    gains = [v.reshape(1, -1) for v in (first_gain, down_gain, third_gain)]
    biases = [v.reshape(1, -1) for v in (first_bias, down_bias, third_bias)]
    unit = 2 * 9 * n * in_chans * CELLS

    slices, weights, kept, up = kernel_call(
        send_kernel,
        (
            struct((2, in_chans, CELLS), jnp.bfloat16),
            struct(first_weight.shape, jnp.bfloat16),
            struct((n, CELLS)),
            struct((2, n, CELLS), jnp.bfloat16),
        ),
        (
            pltpu.with_memory_space_constraint(features, pltpu.HBM),
            pltpu.with_memory_space_constraint(first_weight, pltpu.HBM),
        ),
        4 * unit,
        "send",
        in_specs=[HBM, HBM],
        scratch=[
            pltpu.VMEM(features.shape, jnp.bfloat16),
            pltpu.SemaphoreType.DMA((2,)),
        ],
    )
    got = shift(up, 1)
    own, down, below, stacked = kernel_call(
        own_kernel,
        (
            struct((n, CELLS)),
            struct((n, CELLS)),
            struct((n, CELLS), jnp.float32),
            struct((9, PAIR, 3 * 3 * LANES), jnp.bfloat16),
        ),
        (slices, weights, third_weight),
        2 * unit,
        "own",
    )
    back = shift(below, -1)
    first, copies = kernel_call(
        total_kernel,
        (struct((2, n, CELLS)), struct((2 * chips, LANES))),
        (down, own, got),
        1 << 20,
        "total",
    )
    rows = lax.cond(
        slab() < 2 * chips,
        lambda sent: exchange(sent, ("chip", "core"), turned(2 * chips, 2 * FIRST_CHIP)),
        lambda sent: sent,
        copies,
    )
    parts = kernel_call(
        down_kernel,
        struct((2 * chans * m, HALF_CELLS), jnp.bfloat16),
        (rows, first, kept, back, gains[0], biases[0], jnp.asarray(sampling()), down_weight),
        unit,
        "down",
    )
    parts = exchange(
        parts,
        ("core", "chan"),
        [core * chans + c for core in range(2) for c in turned(chans, FIRST_CHAN)],
    )
    reduced, mine, copies = kernel_call(
        reduced_kernel,
        (struct((2, m, HALF_CELLS)), struct((m, HALF_CELLS)), struct((chips, LANES))),
        (parts,),
        1 << 20,
        "reduced",
    )
    got = across(mine)
    rows = exchange(copies, "chip", turned(chips, SECOND_CHIP))
    copies = kernel_call(
        bottom_kernel,
        struct((chans * 3 * m, HALF_CELLS), jnp.bfloat16),
        (rows, reduced, got, gains[1], biases[1]),
        1 << 20,
        "bottom",
    )
    bottom = exchange(copies, "chan", turned(chans, SECOND_CHAN))
    third, copies = kernel_call(
        third_kernel,
        (struct((m, HALF_CELLS)), struct((2 * chips, LANES))),
        (bottom, stacked),
        unit,
        "third",
    )
    rows = exchange(copies, ("chip", "core"), turned(2 * chips, 2 * THIRD_CHIP))
    out = kernel_call(
        last_kernel,
        struct((m, HALF_CELLS), jnp.bfloat16),
        (rows, third, gains[2], biases[2]),
        1 << 20,
        "last",
    )
    return out.reshape(m, 1, HALF_CELLS)


def solution(mesh):
    chans = mesh.shape["chan"]
    pairs = jax.sharding.Mesh(mesh.devices.reshape(-1, 2, chans), ("chip", "core", "chan"))
    space = ("chip", "core")
    return jax.shard_map(
        local,
        mesh=pairs,
        in_specs=(
            P(None, space, None),
            P(None, "chan", None),
            P("chan"),
            P("chan"),
            P(None, None, "chan"),
            P("chan"),
            P("chan"),
            P(None, "chan", None),
            P("chan"),
            P("chan"),
        ),
        out_specs=P("chan", space, None),
        check_vma=False,
    )
```

```python
import jax
import jax.numpy as jnp
import ml_dtypes
import numpy as np
from jax import lax
from jax.experimental import pallas as pl
from jax.experimental.pallas import tpu as pltpu
from jax.sharding import PartitionSpec as P

ROWS = 16
COLS = 32
CELLS = ROWS * COLS
HALF_ROWS = ROWS // 2
HALF_COLS = COLS // 2
HALF_CELLS = HALF_ROWS * HALF_COLS
LANES = 128
PAIR = 48
FIRST_CHIP = 31
SECOND_CHIP = 7
THIRD_CHIP = 20
FIRST_CHAN = 5
SECOND_CHAN = 5
EPSILON = 1e-05
SLOPE = 0.01

VMEM = pl.BlockSpec(memory_space=pltpu.VMEM)
HBM = pl.BlockSpec(memory_space=pltpu.HBM)


def kernel_call(body, outputs, operands, flops, name, in_specs=None, scratch=()):
    return pl.pallas_call(
        body,
        out_shape=outputs,
        in_specs=in_specs or [VMEM] * len(operands),
        out_specs=jax.tree.map(lambda _: VMEM, outputs),
        scratch_shapes=scratch,
        compiler_params=pltpu.CompilerParams(vmem_limit_bytes=32 * 1024 * 1024),
        cost_estimate=pl.CostEstimate(flops=flops, bytes_accessed=2 << 20, transcendentals=0),
        name=name,
    )(*operands)


def iota(shape, dim):
    return lax.broadcasted_iota(jnp.int32, shape, dim)


def dot(a, b):
    return jnp.dot(a, b, preferred_element_type=jnp.float32)


def to_row(column, offset):
    n = column.shape[0]
    hit = iota((n, LANES), 1) == iota((n, LANES), 0) + offset
    return jnp.sum(jnp.where(hit, column, 0.0), axis=0, keepdims=True)


def to_column(row, offset, n):
    width = row.shape[1]
    hit = iota((n, width), 1) == iota((n, width), 0) + offset
    return jnp.sum(jnp.where(hit, row, 0.0), axis=1, keepdims=True)


def shift_add(taps, out_chans, row_count, col_count):
    cells = row_count * col_count
    block = 3 * out_chans
    cell = iota((block, cells), 1)
    above = pltpu.roll(taps[:block], col_count, axis=1)
    below = pltpu.roll(taps[2 * block :], cells - col_count, axis=1)
    rows = (
        taps[block : 2 * block]
        + jnp.where(cell >= col_count, above, 0.0)
        + jnp.where(cell < cells - col_count, below, 0.0)
    )
    column = iota((out_chans, cells), 1) % col_count
    left = pltpu.roll(rows[:out_chans], 1, axis=1)
    right = pltpu.roll(rows[2 * out_chans :], cells - 1, axis=1)
    return (
        rows[out_chans : 2 * out_chans]
        + jnp.where(column != 0, left, 0.0)
        + jnp.where(column != col_count - 1, right, 0.0)
    )


def leaky(value):
    return jnp.where(value >= 0, value, SLOPE * value)


def send_kernel(
    features_hbm, weight_hbm,
    slices_ref, weight_ref, kept_ref, up_ref,
    features_ref, sems,
):
    loads = [
        pltpu.make_async_copy(features_hbm, features_ref, sems.at[0]),
        pltpu.make_async_copy(weight_hbm, weight_ref, sems.at[1]),
    ]
    for load in loads:
        load.start()
    chans = features_ref.shape[0]
    gap = iota((chans, 2 * chans), 1) - 2 * iota((chans, 2 * chans), 0)
    picks = [(gap == j).astype(jnp.bfloat16) for j in range(2)]
    loads[0].wait()
    pairs = features_ref[...].reshape(2 * chans, CELLS)
    for j in range(2):
        slices_ref[j] = dot(picks[j], pairs).astype(jnp.bfloat16)
    block = weight_ref.shape[0] // 3
    out_chans = block // 9
    lower, upper = slices_ref[0], slices_ref[1]
    loads[1].wait()
    tap0, tap1 = (weight_ref[k * block : (k + 1) * block] for k in range(2))
    up0 = shift_add(dot(tap0, lower) + dot(tap1, upper), out_chans, ROWS, COLS)
    kept_ref[...] = up0
    up_ref[0] = up0.astype(jnp.bfloat16)
    up_ref[1] = shift_add(dot(tap0, upper), out_chans, ROWS, COLS).astype(jnp.bfloat16)


def own_kernel(
    slices_ref, weight_ref, third_ref, own_ref, down_ref, below_ref, stacked_ref
):
    block = weight_ref.shape[0] // 3
    out_chans = block // 9
    lower, upper = slices_ref[0], slices_ref[1]
    tap1, tap2 = weight_ref[block : 2 * block], weight_ref[2 * block :]
    down = shift_add(dot(tap2, lower), out_chans, ROWS, COLS)
    down = jnp.where(slab() == 0, 0.0, down)
    down_ref[...] = down
    below_ref[...] = down.astype(below_ref.dtype)
    own_ref[...] = shift_add(dot(tap1, lower) + dot(tap2, upper), out_chans, ROWS, COLS)

    third_out, third_in = third_ref.shape[1:]
    stacked_ref[...] = jnp.zeros_like(stacked_ref)
    wide = stacked_ref.shape[2] // 3
    for depth in range(3):
        for tap in range(9):
            stacked_ref[tap, :third_out, depth * wide : depth * wide + third_in] = third_ref[
                depth * 9 + tap
            ]


def total_kernel(down_ref, own_ref, got_ref, first_ref, copies_ref):
    got = got_ref[...].astype(jnp.float32)
    first0 = down_ref[...] + got[0]
    first1 = own_ref[...] + jnp.where(slab() == 0, 0.0, got[1])
    first_ref[0] = first0
    first_ref[1] = first1
    cells = 2 * CELLS
    mean = (
        jnp.sum(first0, axis=1, keepdims=True) + jnp.sum(first1, axis=1, keepdims=True)
    ) / cells
    spread = (
        jnp.sum((first0 - mean) ** 2, axis=1, keepdims=True)
        + jnp.sum((first1 - mean) ** 2, axis=1, keepdims=True)
    ) / cells
    row = to_row(mean, 0) + to_row(spread, mean.shape[0])
    copies_ref[...] = jnp.broadcast_to(row, copies_ref.shape)


def column_statistics(rows, n):
    average = jnp.mean(rows, axis=0, keepdims=True)
    apart = jnp.mean((rows - average) ** 2, axis=0, keepdims=True)
    mean = to_column(average, 0, n)
    spread = to_column(average, n, n) + to_column(apart, 0, n)
    return mean, spread


def down_kernel(
    rows_ref, first_ref, kept_ref, back_ref, gain_ref, bias_ref, select_ref, weight_ref,
    parts_ref,
):
    n = first_ref.shape[1]
    mean, spread = column_statistics(rows_ref[...], n)
    gain = to_column(gain_ref[...], 0, n)
    bias = to_column(bias_ref[...], 0, n)
    scale = gain * lax.rsqrt(spread + EPSILON)
    firsts = (first_ref[0], first_ref[1], kept_ref[...] + back_ref[...].astype(jnp.float32))
    levels = [leaky(scale * (first - mean) + bias) for first in firsts]
    levels[0] = jnp.where(slab() == 0, 0.0, levels[0])
    layers = jnp.concatenate(levels, axis=0).astype(jnp.bfloat16)
    out_chans = weight_ref.shape[1]
    picked = dot(layers, select_ref[...]).astype(jnp.bfloat16)
    windows = jnp.concatenate(
        [
            picked[depth * n : (depth + 1) * n, tap * HALF_CELLS : (tap + 1) * HALF_CELLS]
            for depth in range(3)
            for tap in range(9)
        ],
        axis=0,
    )
    parts = lax.dot_general(
        windows, weight_ref[...], (((0,), (0,)), ((), ())), preferred_element_type=jnp.float32
    )
    spare = -out_chans % LANES
    parts = jnp.concatenate([parts, jnp.zeros((HALF_CELLS, spare), jnp.float32)], axis=1).T
    chans = lax.axis_size("chan")
    share = out_chans // chans
    parts = jnp.concatenate(
        [parts[c * share : (c + 1) * share] for c in turned(chans, FIRST_CHAN)], axis=0
    ).astype(jnp.bfloat16)
    for core in range(2):
        parts_ref[core * out_chans : (core + 1) * out_chans] = parts


def own_statistics(value):
    cells = value.shape[1]
    mean = jnp.sum(value, axis=1, keepdims=True) / cells
    spread = jnp.sum((value - mean) ** 2, axis=1, keepdims=True) / cells
    return to_row(mean, 0) + to_row(spread, value.shape[0])


def reduced_kernel(parts_ref, reduced_ref, mine_ref, copies_ref):
    share = reduced_ref.shape[1]
    parts = parts_ref[...].astype(jnp.float32)
    chans = parts.shape[0] // (2 * share)
    totals = []
    for core in range(2):
        shares = [
            parts[(core * chans + c) * share : (core * chans + c + 1) * share]
            for c in range(chans)
        ]
        totals.append(sum(shares[1:], shares[0]))
        reduced_ref[core] = totals[core]
    mine_ref[...] = jnp.where(lax.axis_index("core") == 0, totals[0], totals[1])
    row = own_statistics(jnp.concatenate(totals, axis=1))
    copies_ref[...] = jnp.broadcast_to(row, copies_ref.shape)


def bottom_kernel(rows_ref, reduced_ref, got_ref, gain_ref, bias_ref, copies_ref):
    n = got_ref.shape[0]
    mean, spread = column_statistics(rows_ref[...], n)
    gain = to_column(gain_ref[...], 0, n)
    bias = to_column(bias_ref[...], 0, n)
    scale = gain * lax.rsqrt(spread + EPSILON)
    even = lax.axis_index("core") == 0
    space = slab()
    last = 2 * lax.axis_size("chip") - 1
    got, reduced0, reduced1 = got_ref[...], reduced_ref[0], reduced_ref[1]
    slices = (
        (jnp.where(even, got, reduced0), space != 0),
        (jnp.where(even, reduced0, reduced1), None),
        (jnp.where(even, reduced1, got), space != last),
    )
    bottoms = []
    for value, keep in slices:
        bottom = leaky(scale * (value - mean) + bias)
        bottoms.append(bottom if keep is None else jnp.where(keep, bottom, 0.0))
    copies = jnp.concatenate(bottoms * 2, axis=0).astype(jnp.bfloat16)
    size = copies.shape[0]
    for c in range(copies_ref.shape[0] // size):
        copies_ref[c * size : (c + 1) * size] = copies


def third_kernel(bottom_ref, stacked_ref, third_ref, copies_ref):
    share, cells = third_ref.shape
    depths = 3
    chans = bottom_ref.shape[0] // (depths * share)
    wide = stacked_ref.shape[2] // depths
    gathered = bottom_ref[...].astype(jnp.float32)
    blocks = []
    for k in range(depths):
        for c in turned(chans, chans - SECOND_CHAN):
            at = (c * depths + k) * share
            blocks.append(gathered[at : at + share])
        blocks.append(jnp.zeros((wide - chans * share, cells), jnp.float32))
    bottom = jnp.concatenate(blocks, axis=0).astype(jnp.bfloat16)
    taps = dot(stacked_ref[...].reshape(9 * PAIR, bottom.shape[0]), bottom)
    third = shift_add(taps, PAIR, HALF_ROWS, HALF_COLS)[:share]
    third_ref[...] = third
    copies_ref[...] = jnp.broadcast_to(own_statistics(third), copies_ref.shape)


def last_kernel(rows_ref, third_ref, gain_ref, bias_ref, out_ref):
    n = third_ref.shape[0]
    mean, spread = column_statistics(rows_ref[...], n)
    gain = to_column(gain_ref[...], 0, n)
    bias = to_column(bias_ref[...], 0, n)
    scale = gain * lax.rsqrt(spread + EPSILON)
    out_ref[...] = leaky(scale * (third_ref[...] - mean) + bias).astype(jnp.bfloat16)


def slab():
    return 2 * lax.axis_index("chip") + lax.axis_index("core")


def across(value):
    count = 2 * lax.axis_size("chip")
    pairs = [(i, (i + 2 * (i % 2) - 1) % count) for i in range(count)]
    return lax.ppermute(value, ("chip", "core"), pairs)


def shift(value, by):
    count = 2 * lax.axis_size("chip")
    pairs = [(i, (i + by) % count) for i in range(count)]
    return lax.ppermute(value, ("chip", "core"), pairs)


def turned(count, first):
    return [(first + i) % count for i in range(count)]


def exchange(copies, axes, order):
    return lax.all_to_all(copies, axes, 0, 0, axis_index_groups=[order], tiled=True)


def sampling():
    cell = np.arange(CELLS)[:, None, None]
    tap = np.arange(9)[None, :, None]
    place = np.arange(HALF_CELLS)[None, None, :]
    row = 2 * (place // HALF_COLS) + tap // 3 - 1
    column = 2 * (place % HALF_COLS) + tap % 3 - 1
    hit = (cell // COLS == row) & (cell % COLS == column)
    return hit.reshape(CELLS, 9 * HALF_CELLS).astype(ml_dtypes.bfloat16)


def struct(shape, dtype=jnp.float32):
    return jax.ShapeDtypeStruct(shape, dtype)


def local(
    features,
    first_weight,
    first_gain,
    first_bias,
    down_weight,
    down_gain,
    down_bias,
    third_weight,
    third_gain,
    third_bias,
):
    chips, chans = lax.axis_size("chip"), lax.axis_size("chan")
    in_chans = features.shape[0]
    n = first_weight.shape[1]
    m = third_weight.shape[1]
    wide = down_weight.shape[1]
    first_weight = first_weight.reshape(27 * n, in_chans)
    down_weight = jnp.transpose(down_weight, (0, 2, 1)).reshape(27 * n, wide)
    gains = [v.reshape(1, -1) for v in (first_gain, down_gain, third_gain)]
    biases = [v.reshape(1, -1) for v in (first_bias, down_bias, third_bias)]
    unit = 2 * 9 * n * in_chans * CELLS

    slices, weights, kept, up = kernel_call(
        send_kernel,
        (
            struct((2, in_chans, CELLS), jnp.bfloat16),
            struct(first_weight.shape, jnp.bfloat16),
            struct((n, CELLS)),
            struct((2, n, CELLS), jnp.bfloat16),
        ),
        (
            pltpu.with_memory_space_constraint(features, pltpu.HBM),
            pltpu.with_memory_space_constraint(first_weight, pltpu.HBM),
        ),
        4 * unit,
        "send",
        in_specs=[HBM, HBM],
        scratch=[
            pltpu.VMEM(features.shape, jnp.bfloat16),
            pltpu.SemaphoreType.DMA((2,)),
        ],
    )
    got = shift(up, 1)
    own, down, below, stacked = kernel_call(
        own_kernel,
        (
            struct((n, CELLS)),
            struct((n, CELLS)),
            struct((n, CELLS), jnp.float32),
            struct((9, PAIR, 3 * 3 * LANES), jnp.bfloat16),
        ),
        (slices, weights, third_weight),
        2 * unit,
        "own",
    )
    back = shift(below, -1)
    first, copies = kernel_call(
        total_kernel,
        (struct((2, n, CELLS)), struct((2 * chips, LANES))),
        (down, own, got),
        1 << 20,
        "total",
    )
    rows = lax.cond(
        slab() < 2 * chips,
        lambda sent: exchange(sent, ("chip", "core"), turned(2 * chips, 2 * FIRST_CHIP + 1)),
        lambda sent: sent,
        copies,
    )
    parts = kernel_call(
        down_kernel,
        struct((2 * chans * m, HALF_CELLS), jnp.bfloat16),
        (rows, first, kept, back, gains[0], biases[0], jnp.asarray(sampling()), down_weight),
        unit,
        "down",
    )
    parts = exchange(
        parts,
        ("core", "chan"),
        [core * chans + c for core in range(2) for c in turned(chans, FIRST_CHAN)],
    )
    reduced, mine, copies = kernel_call(
        reduced_kernel,
        (struct((2, m, HALF_CELLS)), struct((m, HALF_CELLS)), struct((chips, LANES))),
        (parts,),
        1 << 20,
        "reduced",
    )
    got = across(mine)
    rows = exchange(copies, "chip", turned(chips, SECOND_CHIP))
    copies = kernel_call(
        bottom_kernel,
        struct((chans * 3 * m, HALF_CELLS), jnp.bfloat16),
        (rows, reduced, got, gains[1], biases[1]),
        1 << 20,
        "bottom",
    )
    bottom = exchange(copies, "chan", turned(chans, SECOND_CHAN))
    third, copies = kernel_call(
        third_kernel,
        (struct((m, HALF_CELLS)), struct((2 * chips, LANES))),
        (bottom, stacked),
        unit,
        "third",
    )
    rows = exchange(copies, ("chip", "core"), turned(2 * chips, 2 * THIRD_CHIP))
    out = kernel_call(
        last_kernel,
        struct((m, HALF_CELLS), jnp.bfloat16),
        (rows, third, gains[2], biases[2]),
        1 << 20,
        "last",
    )
    return out.reshape(m, 1, HALF_CELLS)


def solution(mesh):
    chans = mesh.shape["chan"]
    pairs = jax.sharding.Mesh(mesh.devices.reshape(-1, 2, chans), ("chip", "core", "chan"))
    space = ("chip", "core")
    return jax.shard_map(
        local,
        mesh=pairs,
        in_specs=(
            P(None, space, None),
            P(None, "chan", None),
            P("chan"),
            P("chan"),
            P(None, None, "chan"),
            P("chan"),
            P("chan"),
            P(None, "chan", None),
            P("chan"),
            P("chan"),
        ),
        out_specs=P("chan", space, None),
        check_vma=False,
    )
```

```python
import jax
import jax.numpy as jnp
import ml_dtypes
import numpy as np
from jax import lax
from jax.experimental import pallas as pl
from jax.experimental.pallas import tpu as pltpu
from jax.sharding import PartitionSpec as P

ROWS = 16
COLS = 32
CELLS = ROWS * COLS
HALF_ROWS = ROWS // 2
HALF_COLS = COLS // 2
HALF_CELLS = HALF_ROWS * HALF_COLS
LANES = 128
PAIR = 48
FIRST_CHIP = 31
SECOND_CHIP = 7
THIRD_CHIP = 20
FIRST_CHAN = 5
SECOND_CHAN = 5
EPSILON = 1e-05
SLOPE = 0.01

VMEM = pl.BlockSpec(memory_space=pltpu.VMEM)
HBM = pl.BlockSpec(memory_space=pltpu.HBM)


def kernel_call(body, outputs, operands, flops, name, in_specs=None, scratch=()):
    return pl.pallas_call(
        body,
        out_shape=outputs,
        in_specs=in_specs or [VMEM] * len(operands),
        out_specs=jax.tree.map(lambda _: VMEM, outputs),
        scratch_shapes=scratch,
        compiler_params=pltpu.CompilerParams(vmem_limit_bytes=32 * 1024 * 1024),
        cost_estimate=pl.CostEstimate(flops=flops, bytes_accessed=2 << 20, transcendentals=0),
        name=name,
    )(*operands)


def iota(shape, dim):
    return lax.broadcasted_iota(jnp.int32, shape, dim)


def dot(a, b):
    return jnp.dot(a, b, preferred_element_type=jnp.float32)


def to_row(column, offset):
    n = column.shape[0]
    hit = iota((n, LANES), 1) == iota((n, LANES), 0) + offset
    return jnp.sum(jnp.where(hit, column, 0.0), axis=0, keepdims=True)


def to_column(row, offset, n):
    width = row.shape[1]
    hit = iota((n, width), 1) == iota((n, width), 0) + offset
    return jnp.sum(jnp.where(hit, row, 0.0), axis=1, keepdims=True)


def shift_add(taps, out_chans, row_count, col_count):
    cells = row_count * col_count
    block = 3 * out_chans
    cell = iota((block, cells), 1)
    above = pltpu.roll(taps[:block], col_count, axis=1)
    below = pltpu.roll(taps[2 * block :], cells - col_count, axis=1)
    rows = (
        taps[block : 2 * block]
        + jnp.where(cell >= col_count, above, 0.0)
        + jnp.where(cell < cells - col_count, below, 0.0)
    )
    column = iota((out_chans, cells), 1) % col_count
    left = pltpu.roll(rows[:out_chans], 1, axis=1)
    right = pltpu.roll(rows[2 * out_chans :], cells - 1, axis=1)
    return (
        rows[out_chans : 2 * out_chans]
        + jnp.where(column != 0, left, 0.0)
        + jnp.where(column != col_count - 1, right, 0.0)
    )


def leaky(value):
    return jnp.where(value >= 0, value, SLOPE * value)


def send_kernel(
    features_hbm, weight_hbm,
    slices_ref, weight_ref, kept_ref, up_ref,
    features_ref, sems,
):
    loads = [
        pltpu.make_async_copy(features_hbm, features_ref, sems.at[0]),
        pltpu.make_async_copy(weight_hbm, weight_ref, sems.at[1]),
    ]
    for load in loads:
        load.start()
    chans = features_ref.shape[0]
    gap = iota((chans, 2 * chans), 1) - 2 * iota((chans, 2 * chans), 0)
    picks = [(gap == j).astype(jnp.bfloat16) for j in range(2)]
    loads[0].wait()
    pairs = features_ref[...].reshape(2 * chans, CELLS)
    for j in range(2):
        slices_ref[j] = dot(picks[j], pairs).astype(jnp.bfloat16)
    block = weight_ref.shape[0] // 3
    out_chans = block // 9
    lower, upper = slices_ref[0], slices_ref[1]
    loads[1].wait()
    tap0, tap1 = (weight_ref[k * block : (k + 1) * block] for k in range(2))
    up0 = shift_add(dot(tap0, lower) + dot(tap1, upper), out_chans, ROWS, COLS)
    kept_ref[...] = up0
    up_ref[0] = up0.astype(jnp.bfloat16)
    up_ref[1] = shift_add(dot(tap0, upper), out_chans, ROWS, COLS).astype(jnp.bfloat16)


def own_kernel(
    slices_ref, weight_ref, third_ref, own_ref, down_ref, below_ref, stacked_ref
):
    block = weight_ref.shape[0] // 3
    out_chans = block // 9
    lower, upper = slices_ref[0], slices_ref[1]
    tap1, tap2 = weight_ref[block : 2 * block], weight_ref[2 * block :]
    down = shift_add(dot(tap2, lower), out_chans, ROWS, COLS)
    down = jnp.where(slab() == 0, 0.0, down)
    down_ref[...] = down
    below_ref[...] = down.astype(below_ref.dtype)
    own_ref[...] = shift_add(dot(tap1, lower) + dot(tap2, upper), out_chans, ROWS, COLS)

    third_out, third_in = third_ref.shape[1:]
    stacked_ref[...] = jnp.zeros_like(stacked_ref)
    wide = stacked_ref.shape[2] // 3
    for depth in range(3):
        for tap in range(9):
            stacked_ref[tap, :third_out, depth * wide : depth * wide + third_in] = third_ref[
                depth * 9 + tap
            ]


def total_kernel(down_ref, own_ref, got_ref, first_ref, copies_ref):
    got = got_ref[...].astype(jnp.float32)
    first0 = down_ref[...] + got[0]
    first1 = own_ref[...] + jnp.where(slab() == 0, 0.0, got[1])
    first_ref[0] = first0
    first_ref[1] = first1
    cells = 2 * CELLS
    mean = (
        jnp.sum(first0, axis=1, keepdims=True) + jnp.sum(first1, axis=1, keepdims=True)
    ) / cells
    spread = (
        jnp.sum((first0 - mean) ** 2, axis=1, keepdims=True)
        + jnp.sum((first1 - mean) ** 2, axis=1, keepdims=True)
    ) / cells
    row = to_row(mean, 0) + to_row(spread, mean.shape[0])
    copies_ref[...] = jnp.broadcast_to(row, copies_ref.shape)


def column_statistics(rows, n):
    average = jnp.mean(rows, axis=0, keepdims=True)
    apart = jnp.mean((rows - average) ** 2, axis=0, keepdims=True)
    mean = to_column(average, 0, n)
    spread = to_column(average, n, n) + to_column(apart, 0, n)
    return mean, spread


def down_kernel(
    rows_ref, first_ref, kept_ref, back_ref, gain_ref, bias_ref, select_ref, weight_ref,
    parts_ref,
):
    n = first_ref.shape[1]
    mean, spread = column_statistics(rows_ref[...], n)
    gain = to_column(gain_ref[...], 0, n)
    bias = to_column(bias_ref[...], 0, n)
    scale = gain * lax.rsqrt(spread + EPSILON)
    firsts = (first_ref[0], first_ref[1], kept_ref[...] + back_ref[...].astype(jnp.float32))
    levels = [leaky(scale * (first - mean) + bias) for first in firsts]
    levels[0] = jnp.where(slab() == 0, 0.0, levels[0])
    layers = jnp.concatenate(levels, axis=0).astype(jnp.bfloat16)
    out_chans = weight_ref.shape[1]
    picked = dot(layers, select_ref[...]).astype(jnp.bfloat16)
    windows = jnp.concatenate(
        [
            picked[depth * n : (depth + 1) * n, tap * HALF_CELLS : (tap + 1) * HALF_CELLS]
            for depth in range(3)
            for tap in range(9)
        ],
        axis=0,
    )
    parts = lax.dot_general(
        windows, weight_ref[...], (((0,), (0,)), ((), ())), preferred_element_type=jnp.float32
    )
    spare = -out_chans % LANES
    parts = jnp.concatenate([parts, jnp.zeros((HALF_CELLS, spare), jnp.float32)], axis=1).T
    chans = lax.axis_size("chan")
    share = out_chans // chans
    parts = jnp.concatenate(
        [parts[c * share : (c + 1) * share] for c in turned(chans, FIRST_CHAN)], axis=0
    ).astype(jnp.bfloat16)
    for core in range(2):
        parts_ref[core * out_chans : (core + 1) * out_chans] = parts


def own_statistics(value):
    cells = value.shape[1]
    mean = jnp.sum(value, axis=1, keepdims=True) / cells
    spread = jnp.sum((value - mean) ** 2, axis=1, keepdims=True) / cells
    return to_row(mean, 0) + to_row(spread, value.shape[0])


def reduced_kernel(parts_ref, reduced_ref, mine_ref, copies_ref):
    share = reduced_ref.shape[1]
    parts = parts_ref[...].astype(jnp.float32)
    chans = parts.shape[0] // (2 * share)
    totals = []
    for core in range(2):
        shares = [
            parts[(core * chans + c) * share : (core * chans + c + 1) * share]
            for c in range(chans)
        ]
        totals.append(sum(shares[1:], shares[0]))
        reduced_ref[core] = totals[core]
    mine_ref[...] = jnp.where(lax.axis_index("core") == 0, totals[0], totals[1])
    row = own_statistics(jnp.concatenate(totals, axis=1))
    copies_ref[...] = jnp.broadcast_to(row, copies_ref.shape)


def bottom_kernel(rows_ref, reduced_ref, got_ref, gain_ref, bias_ref, copies_ref):
    n = got_ref.shape[0]
    mean, spread = column_statistics(rows_ref[...], n)
    gain = to_column(gain_ref[...], 0, n)
    bias = to_column(bias_ref[...], 0, n)
    scale = gain * lax.rsqrt(spread + EPSILON)
    even = lax.axis_index("core") == 0
    space = slab()
    last = 2 * lax.axis_size("chip") - 1
    got, reduced0, reduced1 = got_ref[...], reduced_ref[0], reduced_ref[1]
    slices = (
        (jnp.where(even, got, reduced0), space != 0),
        (jnp.where(even, reduced0, reduced1), None),
        (jnp.where(even, reduced1, got), space != last),
    )
    bottoms = []
    for value, keep in slices:
        bottom = leaky(scale * (value - mean) + bias)
        bottoms.append(bottom if keep is None else jnp.where(keep, bottom, 0.0))
    copies = jnp.concatenate(bottoms * 2, axis=0).astype(jnp.bfloat16)
    size = copies.shape[0]
    for c in range(copies_ref.shape[0] // size):
        copies_ref[c * size : (c + 1) * size] = copies


def third_kernel(bottom_ref, stacked_ref, third_ref, copies_ref):
    share, cells = third_ref.shape
    depths = 3
    chans = bottom_ref.shape[0] // (depths * share)
    gathered = bottom_ref[...].astype(jnp.float32)
    blocks = []
    for k in range(depths):
        for c in turned(chans, chans - SECOND_CHAN):
            at = (c * depths + k) * share
            blocks.append(gathered[at : at + share])
    bottom = jnp.concatenate(blocks, axis=0).astype(jnp.bfloat16)
    taps = dot(stacked_ref[...].reshape(9 * PAIR, bottom.shape[0]), bottom)
    third = shift_add(taps, PAIR, HALF_ROWS, HALF_COLS)[:share]
    third_ref[...] = third
    copies_ref[...] = jnp.broadcast_to(own_statistics(third), copies_ref.shape)


def last_kernel(rows_ref, third_ref, gain_ref, bias_ref, out_ref):
    n = third_ref.shape[0]
    mean, spread = column_statistics(rows_ref[...], n)
    gain = to_column(gain_ref[...], 0, n)
    bias = to_column(bias_ref[...], 0, n)
    scale = gain * lax.rsqrt(spread + EPSILON)
    out_ref[...] = leaky(scale * (third_ref[...] - mean) + bias).astype(jnp.bfloat16)


def slab():
    return 2 * lax.axis_index("chip") + lax.axis_index("core")


def across(value):
    count = 2 * lax.axis_size("chip")
    pairs = [(i, (i + 2 * (i % 2) - 1) % count) for i in range(count)]
    return lax.ppermute(value, ("chip", "core"), pairs)


def shift(value, by):
    count = 2 * lax.axis_size("chip")
    pairs = [(i, (i + by) % count) for i in range(count)]
    return lax.ppermute(value, ("chip", "core"), pairs)


def turned(count, first):
    return [(first + i) % count for i in range(count)]


def exchange(copies, axes, order):
    return lax.all_to_all(copies, axes, 0, 0, axis_index_groups=[order], tiled=True)


def sampling():
    cell = np.arange(CELLS)[:, None, None]
    tap = np.arange(9)[None, :, None]
    place = np.arange(HALF_CELLS)[None, None, :]
    row = 2 * (place // HALF_COLS) + tap // 3 - 1
    column = 2 * (place % HALF_COLS) + tap % 3 - 1
    hit = (cell // COLS == row) & (cell % COLS == column)
    return hit.reshape(CELLS, 9 * HALF_CELLS).astype(ml_dtypes.bfloat16)


def struct(shape, dtype=jnp.float32):
    return jax.ShapeDtypeStruct(shape, dtype)


def local(
    features,
    first_weight,
    first_gain,
    first_bias,
    down_weight,
    down_gain,
    down_bias,
    third_weight,
    third_gain,
    third_bias,
):
    chips, chans = lax.axis_size("chip"), lax.axis_size("chan")
    in_chans = features.shape[0]
    n = first_weight.shape[1]
    m = third_weight.shape[1]
    wide = down_weight.shape[1]
    first_weight = first_weight.reshape(27 * n, in_chans)
    down_weight = jnp.transpose(down_weight, (0, 2, 1)).reshape(27 * n, wide)
    gains = [v.reshape(1, -1) for v in (first_gain, down_gain, third_gain)]
    biases = [v.reshape(1, -1) for v in (first_bias, down_bias, third_bias)]
    unit = 2 * 9 * n * in_chans * CELLS

    slices, weights, kept, up = kernel_call(
        send_kernel,
        (
            struct((2, in_chans, CELLS), jnp.bfloat16),
            struct(first_weight.shape, jnp.bfloat16),
            struct((n, CELLS)),
            struct((2, n, CELLS), jnp.bfloat16),
        ),
        (
            pltpu.with_memory_space_constraint(features, pltpu.HBM),
            pltpu.with_memory_space_constraint(first_weight, pltpu.HBM),
        ),
        4 * unit,
        "send",
        in_specs=[HBM, HBM],
        scratch=[
            pltpu.VMEM(features.shape, jnp.bfloat16),
            pltpu.SemaphoreType.DMA((2,)),
        ],
    )
    got = shift(up, 1)
    own, down, below, stacked = kernel_call(
        own_kernel,
        (
            struct((n, CELLS)),
            struct((n, CELLS)),
            struct((n, CELLS), jnp.float32),
            struct((9, PAIR, 3 * wide), jnp.bfloat16),
        ),
        (slices, weights, third_weight),
        2 * unit,
        "own",
    )
    back = shift(below, -1)
    first, copies = kernel_call(
        total_kernel,
        (struct((2, n, CELLS)), struct((2 * chips, LANES))),
        (down, own, got),
        1 << 20,
        "total",
    )
    rows = lax.cond(
        slab() < 2 * chips,
        lambda sent: exchange(sent, ("chip", "core"), turned(2 * chips, 2 * FIRST_CHIP + 1)),
        lambda sent: sent,
        copies,
    )
    parts = kernel_call(
        down_kernel,
        struct((2 * chans * m, HALF_CELLS), jnp.bfloat16),
        (rows, first, kept, back, gains[0], biases[0], jnp.asarray(sampling()), down_weight),
        unit,
        "down",
    )
    parts = exchange(
        parts,
        ("core", "chan"),
        [core * chans + c for core in range(2) for c in turned(chans, FIRST_CHAN)],
    )
    reduced, mine, copies = kernel_call(
        reduced_kernel,
        (struct((2, m, HALF_CELLS)), struct((m, HALF_CELLS)), struct((chips, LANES))),
        (parts,),
        1 << 20,
        "reduced",
    )
    got = across(mine)
    rows = exchange(copies, "chip", turned(chips, SECOND_CHIP))
    copies = kernel_call(
        bottom_kernel,
        struct((chans * 3 * m, HALF_CELLS), jnp.bfloat16),
        (rows, reduced, got, gains[1], biases[1]),
        1 << 20,
        "bottom",
    )
    bottom = exchange(copies, "chan", turned(chans, SECOND_CHAN))
    third, copies = kernel_call(
        third_kernel,
        (struct((m, HALF_CELLS)), struct((2 * chips, LANES))),
        (bottom, stacked),
        unit,
        "third",
    )
    rows = exchange(copies, ("chip", "core"), turned(2 * chips, 2 * THIRD_CHIP))
    out = kernel_call(
        last_kernel,
        struct((m, HALF_CELLS), jnp.bfloat16),
        (rows, third, gains[2], biases[2]),
        1 << 20,
        "last",
    )
    return out.reshape(m, 1, HALF_CELLS)


def solution(mesh):
    chans = mesh.shape["chan"]
    pairs = jax.sharding.Mesh(mesh.devices.reshape(-1, 2, chans), ("chip", "core", "chan"))
    space = ("chip", "core")
    return jax.shard_map(
        local,
        mesh=pairs,
        in_specs=(
            P(None, space, None),
            P(None, "chan", None),
            P("chan"),
            P("chan"),
            P(None, None, "chan"),
            P("chan"),
            P("chan"),
            P(None, "chan", None),
            P("chan"),
            P("chan"),
        ),
        out_specs=P("chan", space, None),
        check_vma=False,
    )
```

```python
import jax
import jax.numpy as jnp
import ml_dtypes
import numpy as np
from jax import lax
from jax.experimental import pallas as pl
from jax.experimental.pallas import tpu as pltpu
from jax.sharding import PartitionSpec as P

ROWS = 16
COLS = 32
CELLS = ROWS * COLS
HALF_ROWS = ROWS // 2
HALF_COLS = COLS // 2
HALF_CELLS = HALF_ROWS * HALF_COLS
LANES = 128
PAIR = 48
FIRST_CHIP = 31
SECOND_CHIP = 7
THIRD_CHIP = 20
FIRST_CHAN = 5
SECOND_CHAN = 5
EPSILON = 1e-05
SLOPE = 0.01

VMEM = pl.BlockSpec(memory_space=pltpu.VMEM)
HBM = pl.BlockSpec(memory_space=pltpu.HBM)


def kernel_call(body, outputs, operands, flops, name, in_specs=None, scratch=()):
    return pl.pallas_call(
        body,
        out_shape=outputs,
        in_specs=in_specs or [VMEM] * len(operands),
        out_specs=jax.tree.map(lambda _: VMEM, outputs),
        scratch_shapes=scratch,
        compiler_params=pltpu.CompilerParams(vmem_limit_bytes=32 * 1024 * 1024),
        cost_estimate=pl.CostEstimate(flops=flops, bytes_accessed=2 << 20, transcendentals=0),
        name=name,
    )(*operands)


def iota(shape, dim):
    return lax.broadcasted_iota(jnp.int32, shape, dim)


def dot(a, b):
    return jnp.dot(a, b, preferred_element_type=jnp.float32)


def to_row(column, offset):
    n = column.shape[0]
    hit = iota((n, LANES), 1) == iota((n, LANES), 0) + offset
    return jnp.sum(jnp.where(hit, column, 0.0), axis=0, keepdims=True)


def to_column(row, offset, n):
    width = row.shape[1]
    hit = iota((n, width), 1) == iota((n, width), 0) + offset
    return jnp.sum(jnp.where(hit, row, 0.0), axis=1, keepdims=True)


def shift_add(taps, out_chans, row_count, col_count):
    cells = row_count * col_count
    block = 3 * out_chans
    cell = iota((block, cells), 1)
    above = pltpu.roll(taps[:block], col_count, axis=1)
    below = pltpu.roll(taps[2 * block :], cells - col_count, axis=1)
    rows = (
        taps[block : 2 * block]
        + jnp.where(cell >= col_count, above, 0.0)
        + jnp.where(cell < cells - col_count, below, 0.0)
    )
    column = iota((out_chans, cells), 1) % col_count
    left = pltpu.roll(rows[:out_chans], 1, axis=1)
    right = pltpu.roll(rows[2 * out_chans :], cells - 1, axis=1)
    return (
        rows[out_chans : 2 * out_chans]
        + jnp.where(column != 0, left, 0.0)
        + jnp.where(column != col_count - 1, right, 0.0)
    )


def leaky(value):
    return jnp.where(value >= 0, value, SLOPE * value)


def send_kernel(
    features_hbm, weight_hbm,
    slices_ref, weight_ref, kept_ref, up_ref,
    features_ref, sems,
):
    chans = features_ref.shape[0]
    half = chans // 2
    parts = [slice(0, half), slice(half, chans)]
    loads = [
        pltpu.make_async_copy(features_hbm.at[part], features_ref.at[part], sems.at[k])
        for k, part in enumerate(parts)
    ]
    loads.append(pltpu.make_async_copy(weight_hbm, weight_ref, sems.at[2]))
    for load in loads:
        load.start()
    gap = iota((half, chans), 1) - 2 * iota((half, chans), 0)
    picks = [(gap == j).astype(jnp.bfloat16) for j in range(2)]
    for load, part in zip(loads, parts):
        load.wait()
        pairs = features_ref[part].reshape(chans, CELLS)
        for j in range(2):
            slices_ref[j, part] = dot(picks[j], pairs).astype(jnp.bfloat16)
    block = weight_ref.shape[0] // 3
    out_chans = block // 9
    lower, upper = slices_ref[0], slices_ref[1]
    loads[2].wait()
    tap0, tap1 = (weight_ref[k * block : (k + 1) * block] for k in range(2))
    up0 = shift_add(dot(tap0, lower) + dot(tap1, upper), out_chans, ROWS, COLS)
    kept_ref[...] = up0
    up_ref[0] = up0.astype(jnp.bfloat16)
    up_ref[1] = shift_add(dot(tap0, upper), out_chans, ROWS, COLS).astype(jnp.bfloat16)


def own_kernel(
    slices_ref, weight_ref, third_ref, own_ref, down_ref, below_ref, stacked_ref
):
    block = weight_ref.shape[0] // 3
    out_chans = block // 9
    lower, upper = slices_ref[0], slices_ref[1]
    tap1, tap2 = weight_ref[block : 2 * block], weight_ref[2 * block :]
    down = shift_add(dot(tap2, lower), out_chans, ROWS, COLS)
    down = jnp.where(slab() == 0, 0.0, down)
    down_ref[...] = down
    below_ref[...] = down.astype(below_ref.dtype)
    own_ref[...] = shift_add(dot(tap1, lower) + dot(tap2, upper), out_chans, ROWS, COLS)

    third_out, third_in = third_ref.shape[1:]
    stacked_ref[...] = jnp.zeros_like(stacked_ref)
    wide = stacked_ref.shape[2] // 3
    for depth in range(3):
        for tap in range(9):
            stacked_ref[tap, :third_out, depth * wide : depth * wide + third_in] = third_ref[
                depth * 9 + tap
            ]


def total_kernel(down_ref, own_ref, got_ref, first_ref, copies_ref):
    got = got_ref[...].astype(jnp.float32)
    first0 = down_ref[...] + got[0]
    first1 = own_ref[...] + jnp.where(slab() == 0, 0.0, got[1])
    first_ref[0] = first0
    first_ref[1] = first1
    cells = 2 * CELLS
    mean = (
        jnp.sum(first0, axis=1, keepdims=True) + jnp.sum(first1, axis=1, keepdims=True)
    ) / cells
    spread = (
        jnp.sum((first0 - mean) ** 2, axis=1, keepdims=True)
        + jnp.sum((first1 - mean) ** 2, axis=1, keepdims=True)
    ) / cells
    row = to_row(mean, 0) + to_row(spread, mean.shape[0])
    copies_ref[...] = jnp.broadcast_to(row, copies_ref.shape)


def column_statistics(rows, n):
    average = jnp.mean(rows, axis=0, keepdims=True)
    apart = jnp.mean((rows - average) ** 2, axis=0, keepdims=True)
    mean = to_column(average, 0, n)
    spread = to_column(average, n, n) + to_column(apart, 0, n)
    return mean, spread


def down_kernel(
    rows_ref, first_ref, kept_ref, back_ref, gain_ref, bias_ref, select_ref, weight_ref,
    parts_ref,
):
    n = first_ref.shape[1]
    mean, spread = column_statistics(rows_ref[...], n)
    gain = to_column(gain_ref[...], 0, n)
    bias = to_column(bias_ref[...], 0, n)
    scale = gain * lax.rsqrt(spread + EPSILON)
    firsts = (first_ref[0], first_ref[1], kept_ref[...] + back_ref[...].astype(jnp.float32))
    levels = [leaky(scale * (first - mean) + bias) for first in firsts]
    levels[0] = jnp.where(slab() == 0, 0.0, levels[0])
    layers = jnp.concatenate(levels, axis=0).astype(jnp.bfloat16)
    out_chans = weight_ref.shape[1]
    picked = dot(layers, select_ref[...]).astype(jnp.bfloat16)
    windows = jnp.concatenate(
        [
            picked[depth * n : (depth + 1) * n, tap * HALF_CELLS : (tap + 1) * HALF_CELLS]
            for depth in range(3)
            for tap in range(9)
        ],
        axis=0,
    )
    parts = lax.dot_general(
        windows, weight_ref[...], (((0,), (0,)), ((), ())), preferred_element_type=jnp.float32
    )
    spare = -out_chans % LANES
    parts = jnp.concatenate([parts, jnp.zeros((HALF_CELLS, spare), jnp.float32)], axis=1).T
    chans = lax.axis_size("chan")
    share = out_chans // chans
    parts = jnp.concatenate(
        [parts[c * share : (c + 1) * share] for c in turned(chans, FIRST_CHAN)], axis=0
    ).astype(jnp.bfloat16)
    for core in range(2):
        parts_ref[core * out_chans : (core + 1) * out_chans] = parts


def own_statistics(value):
    cells = value.shape[1]
    mean = jnp.sum(value, axis=1, keepdims=True) / cells
    spread = jnp.sum((value - mean) ** 2, axis=1, keepdims=True) / cells
    return to_row(mean, 0) + to_row(spread, value.shape[0])


def reduced_kernel(parts_ref, reduced_ref, mine_ref, copies_ref):
    share = reduced_ref.shape[1]
    parts = parts_ref[...].astype(jnp.float32)
    chans = parts.shape[0] // (2 * share)
    totals = []
    for core in range(2):
        shares = [
            parts[(core * chans + c) * share : (core * chans + c + 1) * share]
            for c in range(chans)
        ]
        totals.append(sum(shares[1:], shares[0]))
        reduced_ref[core] = totals[core]
    mine_ref[...] = jnp.where(lax.axis_index("core") == 0, totals[0], totals[1])
    row = own_statistics(jnp.concatenate(totals, axis=1))
    copies_ref[...] = jnp.broadcast_to(row, copies_ref.shape)


def bottom_kernel(rows_ref, reduced_ref, got_ref, gain_ref, bias_ref, copies_ref):
    n = got_ref.shape[0]
    mean, spread = column_statistics(rows_ref[...], n)
    gain = to_column(gain_ref[...], 0, n)
    bias = to_column(bias_ref[...], 0, n)
    scale = gain * lax.rsqrt(spread + EPSILON)
    even = lax.axis_index("core") == 0
    space = slab()
    last = 2 * lax.axis_size("chip") - 1
    got, reduced0, reduced1 = got_ref[...], reduced_ref[0], reduced_ref[1]
    slices = (
        (jnp.where(even, got, reduced0), space != 0),
        (jnp.where(even, reduced0, reduced1), None),
        (jnp.where(even, reduced1, got), space != last),
    )
    bottoms = []
    for value, keep in slices:
        bottom = leaky(scale * (value - mean) + bias)
        bottoms.append(bottom if keep is None else jnp.where(keep, bottom, 0.0))
    copies = jnp.concatenate(bottoms * 2, axis=0).astype(jnp.bfloat16)
    size = copies.shape[0]
    for c in range(copies_ref.shape[0] // size):
        copies_ref[c * size : (c + 1) * size] = copies


def third_kernel(bottom_ref, stacked_ref, third_ref, copies_ref):
    share, cells = third_ref.shape
    depths = 3
    chans = bottom_ref.shape[0] // (depths * share)
    gathered = bottom_ref[...].astype(jnp.float32)
    blocks = []
    for k in range(depths):
        for c in turned(chans, chans - SECOND_CHAN):
            at = (c * depths + k) * share
            blocks.append(gathered[at : at + share])
    bottom = jnp.concatenate(blocks, axis=0).astype(jnp.bfloat16)
    taps = dot(stacked_ref[...].reshape(9 * PAIR, bottom.shape[0]), bottom)
    third = shift_add(taps, PAIR, HALF_ROWS, HALF_COLS)[:share]
    third_ref[...] = third
    copies_ref[...] = jnp.broadcast_to(own_statistics(third), copies_ref.shape)


def last_kernel(rows_ref, third_ref, gain_ref, bias_ref, out_ref):
    n = third_ref.shape[0]
    mean, spread = column_statistics(rows_ref[...], n)
    gain = to_column(gain_ref[...], 0, n)
    bias = to_column(bias_ref[...], 0, n)
    scale = gain * lax.rsqrt(spread + EPSILON)
    out_ref[...] = leaky(scale * (third_ref[...] - mean) + bias).astype(jnp.bfloat16)


def slab():
    return 2 * lax.axis_index("chip") + lax.axis_index("core")


def across(value):
    count = 2 * lax.axis_size("chip")
    pairs = [(i, (i + 2 * (i % 2) - 1) % count) for i in range(count)]
    return lax.ppermute(value, ("chip", "core"), pairs)


def shift(value, by):
    count = 2 * lax.axis_size("chip")
    pairs = [(i, (i + by) % count) for i in range(count)]
    return lax.ppermute(value, ("chip", "core"), pairs)


def turned(count, first):
    return [(first + i) % count for i in range(count)]


def exchange(copies, axes, order):
    return lax.all_to_all(copies, axes, 0, 0, axis_index_groups=[order], tiled=True)


def sampling():
    cell = np.arange(CELLS)[:, None, None]
    tap = np.arange(9)[None, :, None]
    place = np.arange(HALF_CELLS)[None, None, :]
    row = 2 * (place // HALF_COLS) + tap // 3 - 1
    column = 2 * (place % HALF_COLS) + tap % 3 - 1
    hit = (cell // COLS == row) & (cell % COLS == column)
    return hit.reshape(CELLS, 9 * HALF_CELLS).astype(ml_dtypes.bfloat16)


def struct(shape, dtype=jnp.float32):
    return jax.ShapeDtypeStruct(shape, dtype)


def local(
    features,
    first_weight,
    first_gain,
    first_bias,
    down_weight,
    down_gain,
    down_bias,
    third_weight,
    third_gain,
    third_bias,
):
    chips, chans = lax.axis_size("chip"), lax.axis_size("chan")
    in_chans = features.shape[0]
    n = first_weight.shape[1]
    m = third_weight.shape[1]
    wide = down_weight.shape[1]
    first_weight = first_weight.reshape(27 * n, in_chans)
    down_weight = jnp.transpose(down_weight, (0, 2, 1)).reshape(27 * n, wide)
    gains = [v.reshape(1, -1) for v in (first_gain, down_gain, third_gain)]
    biases = [v.reshape(1, -1) for v in (first_bias, down_bias, third_bias)]
    unit = 2 * 9 * n * in_chans * CELLS

    slices, weights, kept, up = kernel_call(
        send_kernel,
        (
            struct((2, in_chans, CELLS), jnp.bfloat16),
            struct(first_weight.shape, jnp.bfloat16),
            struct((n, CELLS)),
            struct((2, n, CELLS), jnp.bfloat16),
        ),
        (
            pltpu.with_memory_space_constraint(features, pltpu.HBM),
            pltpu.with_memory_space_constraint(first_weight, pltpu.HBM),
        ),
        4 * unit,
        "send",
        in_specs=[HBM, HBM],
        scratch=[
            pltpu.VMEM(features.shape, jnp.bfloat16),
            pltpu.SemaphoreType.DMA((3,)),
        ],
    )
    got = shift(up, 1)
    own, down, below, stacked = kernel_call(
        own_kernel,
        (
            struct((n, CELLS)),
            struct((n, CELLS)),
            struct((n, CELLS), jnp.float32),
            struct((9, PAIR, 3 * wide), jnp.bfloat16),
        ),
        (slices, weights, third_weight),
        2 * unit,
        "own",
    )
    back = shift(below, -1)
    first, copies = kernel_call(
        total_kernel,
        (struct((2, n, CELLS)), struct((2 * chips, LANES))),
        (down, own, got),
        1 << 20,
        "total",
    )
    rows = lax.cond(
        slab() < 2 * chips,
        lambda sent: exchange(sent, ("chip", "core"), turned(2 * chips, 2 * FIRST_CHIP + 1)),
        lambda sent: sent,
        copies,
    )
    parts = kernel_call(
        down_kernel,
        struct((2 * chans * m, HALF_CELLS), jnp.bfloat16),
        (rows, first, kept, back, gains[0], biases[0], jnp.asarray(sampling()), down_weight),
        unit,
        "down",
    )
    parts = exchange(
        parts,
        ("core", "chan"),
        [core * chans + c for core in range(2) for c in turned(chans, FIRST_CHAN)],
    )
    reduced, mine, copies = kernel_call(
        reduced_kernel,
        (struct((2, m, HALF_CELLS)), struct((m, HALF_CELLS)), struct((chips, LANES))),
        (parts,),
        1 << 20,
        "reduced",
    )
    got = across(mine)
    rows = exchange(copies, "chip", turned(chips, SECOND_CHIP))
    copies = kernel_call(
        bottom_kernel,
        struct((chans * 3 * m, HALF_CELLS), jnp.bfloat16),
        (rows, reduced, got, gains[1], biases[1]),
        1 << 20,
        "bottom",
    )
    bottom = exchange(copies, "chan", turned(chans, SECOND_CHAN))
    third, copies = kernel_call(
        third_kernel,
        (struct((m, HALF_CELLS)), struct((2 * chips, LANES))),
        (bottom, stacked),
        unit,
        "third",
    )
    rows = exchange(copies, ("chip", "core"), turned(2 * chips, 2 * THIRD_CHIP))
    out = kernel_call(
        last_kernel,
        struct((m, HALF_CELLS), jnp.bfloat16),
        (rows, third, gains[2], biases[2]),
        1 << 20,
        "last",
    )
    return out.reshape(m, 1, HALF_CELLS)


def solution(mesh):
    chans = mesh.shape["chan"]
    pairs = jax.sharding.Mesh(mesh.devices.reshape(-1, 2, chans), ("chip", "core", "chan"))
    space = ("chip", "core")
    return jax.shard_map(
        local,
        mesh=pairs,
        in_specs=(
            P(None, space, None),
            P(None, "chan", None),
            P("chan"),
            P("chan"),
            P(None, None, "chan"),
            P("chan"),
            P("chan"),
            P(None, "chan", None),
            P("chan"),
            P("chan"),
        ),
        out_specs=P("chan", space, None),
        check_vma=False,
    )
```
